256 devices in a mesh: dom: 64 (over y, x_hi, z), cls: 4 (over x_lo, core).
Axes of the slice: x: 4 (x_hi: 2, x_lo: 2; x = x_hi * 2 + x_lo), y: 4, z: 8, core: 2. Of those that a mesh axis runs over, the one named last changes fastest.
Arguments:
- images: bfloat16 [4096, 3072], P('dom'), may hold values from -160 to 160
- offsets: int32 [4096, 2], P('dom'), may hold values from -4 to 4
- class_lists: int32 [4096, 8], P('dom'), may hold values from 0 to 99, as said below
- noise_weight: float32 [1536], replicated, may hold values from 0.5 to 2
- references: bfloat16 [100, 24, 3072], P('cls', None, 'dom'), may hold values from -3 to 3
Outputs:
- class_sums: float32 [3072, 2400], P('dom', 'cls')
The draws below stay inside these ranges and needn't reach their ends.
Inputs may be any that keep to these rules, and one draw needn't show every extreme that they name: `class_lists`: each particle names 8 different classes.
All inputs are finite; a program needn't handle non-finite values.
Results may differ from the reference program's by a relative error of at most 0.0023.
Values may be sent and summed in bfloat16 or wider, within the bound.
No kernel may reach another device: no remote copies, remote signals or barrier semaphores. Data moves between devices by JAX's collectives and lax.ppermute only.
A program may use at most 128 MiB of HBM per device.

```python
import math
import jax
import jax.numpy as jnp
from jax import lax

K = 1536
C = 100
R = 24
GRID = 5
BOX = 64
NSIG = 8
P_DEV = 64
NPART = 4096
N_DOM = 64


def shared_draw(key):
    key_offset = jax.random.fold_in(key, 101)
    key_lists = jax.random.fold_in(key, 102)
    key_refs = jax.random.fold_in(key, 103)
    offsets = jax.random.randint(key_offset, (NPART, 2), -4, 5).astype(jnp.int32)
    ranking = jax.random.randint(key_lists, (NPART, C), 0, 1 << 20).astype(jnp.int32) * C + jnp.arange(C, dtype=jnp.int32)[None, :]
    class_lists = jnp.argsort(ranking, axis=1)[:, :NSIG].astype(jnp.int32)
    refs = 0.5 * jnp.clip(jax.random.normal(key_refs, (C, R, 2 * K), jnp.float32), -6.0, 6.0)
    return (offsets, class_lists, refs)


def draw_offsets(key, part):
    offsets, class_lists, refs = shared_draw(key)
    return offsets


def draw_class_lists(key, part):
    offsets, class_lists, refs = shared_draw(key)
    return class_lists


def draw_references(key, part):
    offsets, class_lists, refs = shared_draw(key)
    return refs.astype(jnp.bfloat16)


def draw_images(key, part):
    offsets, class_lists, refs = shared_draw(key)
    noise = jnp.clip(jax.random.normal(jax.random.fold_in(key, 104), (NPART, 2 * K), jnp.float32), -6.0, 6.0)
    row_index = jnp.arange(NPART, dtype=jnp.int32)
    aligned = row_index % 16 == 3
    target = (120 + 60 * (row_index // 16 % 3)).astype(jnp.float32)
    strength = 0.5 + target * math.sqrt(2 * K) / (0.27 * 2 * K)
    picked = refs[class_lists[:, 0], row_index % R]
    coeff_index = jnp.arange(K, dtype=jnp.int32)
    freq_x = (coeff_index % BOX - BOX // 2).astype(jnp.float32)
    freq_y = (coeff_index // BOX).astype(jnp.float32)
    angles = 2.0 * math.pi / BOX * (offsets[:, 0:1].astype(jnp.float32) * freq_x[None, :] + offsets[:, 1:2].astype(jnp.float32) * freq_y[None, :])
    cosine = jnp.cos(angles)
    sine_part = jnp.sin(angles)
    ref_re = picked[:, :K]
    ref_im = picked[:, K:]
    image_re = ref_re * cosine - ref_im * sine_part
    image_im = ref_im * cosine + ref_re * sine_part
    matched = jnp.clip(strength[:, None] * jnp.concatenate([image_re, image_im], axis=1), -160.0, 160.0)
    result = jnp.where(aligned[:, None], matched, noise)
    return result.astype(jnp.bfloat16)


def setup_inputs(seed: int = 0) -> dict:
    arg_keys = jax.random.split(jax.random.key(seed), 6)
    return {
        "images": draw_images(jax.random.fold_in(arg_keys[5], 71), 0),
        "offsets": draw_offsets(jax.random.fold_in(arg_keys[5], 71), 0),
        "class_lists": draw_class_lists(jax.random.fold_in(arg_keys[5], 71), 0),
        "noise_weight": jnp.clip(jnp.exp(jax.random.uniform(arg_keys[3], (K,), jnp.float32, math.log(0.5), math.log(2.0))), 0.5, 2.0),
        "references": draw_references(jax.random.fold_in(arg_keys[5], 71), 0),
    }


excluded = -1e+30

def probe_images(images, offsets, noise_weight):
    half_width = images.shape[1] // 2
    shifts = GRID * GRID
    coeff_index = jnp.arange(half_width, dtype=jnp.int32)
    freq_x = (coeff_index % BOX - BOX // 2).astype(jnp.float32)
    freq_y = (coeff_index // BOX).astype(jnp.float32)
    shift_index = jnp.arange(shifts, dtype=jnp.int32)
    grid_x = shift_index % GRID - GRID // 2
    grid_y = shift_index // GRID - GRID // 2
    move_x = (offsets[:, 0:1] + grid_x[None, :]).astype(jnp.float32)
    move_y = (offsets[:, 1:2] + grid_y[None, :]).astype(jnp.float32)
    angles = 2.0 * math.pi / BOX * (move_x[:, :, None] * freq_x[None, None, :] + move_y[:, :, None] * freq_y[None, None, :])
    cosine = jnp.cos(angles)
    sine_part = jnp.sin(angles)
    values = images.astype(jnp.float32)
    real_part = values[:, None, :half_width]
    imag_part = values[:, None, half_width:]
    shifted_re = (real_part * cosine + imag_part * sine_part) * noise_weight
    shifted_im = (imag_part * cosine - real_part * sine_part) * noise_weight
    return jnp.concatenate([shifted_re, shifted_im], axis=-1).astype(jnp.bfloat16)

def reference(images, offsets, class_lists, noise_weight, references):
    width = images.shape[1]
    shifts = GRID * GRID
    flat_refs = references.reshape(C * R, width).astype(jnp.float32)
    weight_cols = jnp.concatenate([noise_weight, noise_weight])
    energy = jnp.dot(flat_refs * flat_refs, weight_cols, precision=lax.Precision.HIGHEST)
    scale_factor = 1.0 / math.sqrt(width)
    class_ids = jnp.arange(C, dtype=jnp.int32)

    def one_block(totals, block):
        block_images, block_offsets, block_lists = block
        rows = block_images.shape[0]
        probes = probe_images(block_images, block_offsets, noise_weight)
        probe_rows = probes.reshape(rows * shifts, width).astype(jnp.float32)
        cross = jnp.dot(probe_rows, flat_refs.T, precision=lax.Precision.HIGHEST)
        scores = ((cross - 0.5 * energy[None, :]) * scale_factor).reshape(rows, shifts, C, R)
        listed = jnp.any(block_lists[:, :, None] == class_ids[None, None, :], axis=1)
        keep = listed[:, None, :, None]
        masked = jnp.where(keep, scores, excluded)
        top_score = lax.optimization_barrier(jnp.max(masked, axis=(1, 2, 3)))
        expo = jnp.where(keep, jnp.exp(masked - top_score[:, None, None, None]), 0.0)
        mass_total = lax.optimization_barrier(jnp.sum(expo, axis=(1, 2, 3)))
        posterior = (expo / mass_total[:, None, None, None]).astype(jnp.bfloat16)
        post_rows = posterior.reshape(rows * shifts, C * R).astype(jnp.float32)
        totals = totals + jnp.dot(probe_rows.T, post_rows, precision=lax.Precision.HIGHEST)
        return (totals, None)
    blocks = (images.reshape(N_DOM, P_DEV, width), offsets.reshape(N_DOM, P_DEV, 2), class_lists.reshape(N_DOM, P_DEV, NSIG))
    start_totals = jnp.zeros((width, C * R), jnp.float32)
    totals, unused = lax.scan(one_block, start_totals, blocks)
    return totals
```

```python
import functools
import math

import jax
import jax.numpy as jnp
import numpy as np
from jax import lax
from jax.experimental import pallas as pl
from jax.experimental.pallas import tpu as pltpu
from jax.sharding import Mesh, PartitionSpec as P

GRID = 5
BOX = 64
HALF = 1536
WIDTH = 3072
PARTS = 64
ROWS = 75
PAD = 80
LANES = 128
CHUNK = 384
GROUP = 8
NPART = PARTS * GROUP
SHIFTS = GRID * GRID
EXCLUDED = -1e30
SCALE = 1.0 / math.sqrt(WIDTH)
AXES = ("y", "xh", "z", "xl", "co")

f32 = jnp.float32
bf16 = jnp.bfloat16


def twiddles():
    k = np.arange(HALF)
    kx = k % BOX - BOX // 2
    ky = k // BOX
    rows = []
    for freq in (kx, ky):
        for g in (1, 2):
            angle = 2.0 * math.pi / BOX * ((g * freq) % BOX)
            rows += [np.cos(angle), np.sin(angle)]
    return np.stack(rows).astype(np.float32)


def sin_cos(turns):
    quarter = jnp.floor(turns * (1.0 / 16.0) + 0.5)
    rest = (turns - 16.0 * quarter) * (2.0 * math.pi / BOX)
    sq = rest * rest
    sin = rest * (
        1.0 + sq * (-1.0 / 6 + sq * (1.0 / 120 + sq * (-1.0 / 5040 + sq * (1.0 / 362880))))
    )
    cos = 1.0 + sq * (
        -0.5 + sq * (1.0 / 24 + sq * (-1.0 / 720 + sq * (1.0 / 40320 + sq * (-1.0 / 3628800))))
    )
    quad = quarter - 4.0 * jnp.floor(quarter * 0.25)
    swap = (quad == 1.0) | (quad == 3.0)
    sin_q = jnp.where(swap, cos, sin)
    cos_q = jnp.where(swap, sin, cos)
    sin_q = jnp.where(quad >= 2.0, -sin_q, sin_q)
    cos_q = jnp.where((quad == 1.0) | (quad == 2.0), -cos_q, cos_q)
    return sin_q, cos_q


def prep_kernel(img_ref, off_ref, list_ref, w_ref, out_ref):
    off = off_ref[...].astype(f32)
    ox, oy = off[:, 0:1], off[:, 1:2]
    for t in range(HALF // LANES):
        lanes = slice(t * LANES, (t + 1) * LANES)
        k = lax.broadcasted_iota(jnp.int32, (1, LANES), 1) + t * LANES
        kx = ((k & (BOX - 1)) - BOX // 2).astype(f32)
        ky = (k >> 6).astype(f32)
        sin, cos = sin_cos(ox * kx + oy * ky)
        a = img_ref[:, lanes].astype(f32)
        b = img_ref[:, HALF + t * LANES : HALF + (t + 1) * LANES].astype(f32)
        w = w_ref[:, lanes]
        out_ref[:, lanes] = (w * (a * cos + b * sin)).astype(bf16)
        out_ref[:, HALF + t * LANES : HALF + (t + 1) * LANES] = (w * (b * cos - a * sin)).astype(
            bf16
        )
    lists = list_ref[...]
    lane = lax.broadcasted_iota(jnp.int32, (PARTS, LANES), 1)
    listed = lists[:, 0:1] == lane
    for n in range(1, lists.shape[1]):
        listed = listed | (lists[:, n : n + 1] == lane)
    out_ref[:, WIDTH:] = jnp.where(listed, 1.0, 0.0).astype(bf16)


def prep(images, offsets, class_lists, weight):
    return pl.pallas_call(
        prep_kernel,
        out_shape=jax.ShapeDtypeStruct((PARTS, WIDTH + LANES), bf16),
    )(images, offsets, class_lists, weight)


def rotate_x(yr, yi, tab_ref, g, lanes):
    c = tab_ref[2 * g - 2 : 2 * g - 1, lanes]
    s = tab_ref[2 * g - 1 : 2 * g, lanes]
    cr, ci, sr, si = yr * c, yi * c, yr * s, yi * s
    return (cr - si, ci + sr), (cr + si, ci - sr)


def y_twiddle(tab_ref, step, lanes):
    two = (step == 0) | (step == 4)
    zero = step == 2
    sign = jnp.where(step < 2, -1.0, 1.0)
    c = jnp.where(two, tab_ref[6:7, lanes], tab_ref[4:5, lanes])
    s = jnp.where(two, tab_ref[7:8, lanes], tab_ref[5:6, lanes])
    return jnp.where(zero, 1.0, c), jnp.where(zero, 0.0, s * sign)


def estep_kernel(base_ref, p_ref, r_ref, tab_ref, w_ref, expo_ref, stat_ref, shifted, energy, mask, top):
    step = pl.program_id(0)

    @pl.when(step == 0)
    def _():
        total = jnp.zeros((PAD, LANES), f32)
        for g in range(GROUP):
            for t in range(CHUNK // LANES):
                r = r_ref[g, :, t * LANES : (t + 1) * LANES].astype(f32)
                at = (g % 4) * CHUNK + t * LANES
                total = total + r * r * w_ref[:, at : at + LANES]
        energy[...] = jnp.broadcast_to(0.5 * jnp.sum(total, axis=1, keepdims=True), energy.shape)
        row = lax.broadcasted_iota(jnp.int32, (PAD, LANES), 0)
        number = ((base_ref[0] + row) * 2731) >> 16
        lane = lax.broadcasted_iota(jnp.int32, (PAD, LANES), 1)
        pick = jnp.where((number == lane) & (row < ROWS), 1.0, 0.0).astype(bf16)
        mask[...] = lax.dot_general(
            pick, p_ref[:, WIDTH:], (((1,), (1,)), ((), ())), preferred_element_type=f32
        )
        top[...] = jnp.full(top.shape, EXCLUDED, f32)

    for g in range(4):
        for t in range(CHUNK // LANES):
            at = g * CHUNK + t * LANES
            lanes = slice(at, at + LANES)
            ims = slice(HALF + at, HALF + at + LANES)
            rr = r_ref[g, :, t * LANES : (t + 1) * LANES].astype(f32)
            ri = r_ref[g + 4, :, t * LANES : (t + 1) * LANES].astype(f32)
            cy, sy = y_twiddle(tab_ref, step, lanes)
            yr = rr * cy - ri * sy
            yi = ri * cy + rr * sy
            shifted[2 * PAD : 3 * PAD, lanes] = yr.astype(bf16)
            shifted[2 * PAD : 3 * PAD, ims] = yi.astype(bf16)
            for gx in (1, 2):
                plus, minus = rotate_x(yr, yi, tab_ref, gx, lanes)
                for at_row, (vr, vi) in (((2 + gx) * PAD, plus), ((2 - gx) * PAD, minus)):
                    shifted[at_row : at_row + PAD, lanes] = vr.astype(bf16)
                    shifted[at_row : at_row + PAD, ims] = vi.astype(bf16)
    cross = lax.dot_general(
        shifted[...], p_ref[:, :WIDTH], (((1,), (1,)), ((), ())), preferred_element_type=f32
    )
    half_energy = energy[:, 0:1]
    keep = mask[...] > 0.5
    best = top[...]
    for gx in range(GRID):
        score = (cross[gx * PAD : (gx + 1) * PAD] - half_energy) * SCALE
        score = jnp.where(keep, score, EXCLUDED)
        expo_ref[pl.ds(pl.multiple_of((step * GRID + gx) * PAD, PAD), PAD), :] = score
        best = jnp.maximum(best, jnp.max(score.reshape(PAD // 8, 8, NPART), axis=0))
    top[...] = best

    @pl.when(step == GRID - 1)
    def _():
        peak = jnp.max(top[...], axis=0, keepdims=True)

        def body(s, mass):
            at = pl.ds(pl.multiple_of(s * PAD, PAD), PAD)
            e = jnp.where(mask[...] > 0.5, jnp.exp(expo_ref[at, :] - peak), 0.0)
            expo_ref[at, :] = e
            return mass + jnp.sum(e.reshape(PAD // 8, 8, NPART), axis=0)

        mass = lax.fori_loop(0, SHIFTS, body, jnp.zeros((8, NPART), f32))
        stat_ref[0:1, :] = peak
        stat_ref[1:2, :] = jnp.sum(mass, axis=0, keepdims=True)


def full(shape):
    return pl.BlockSpec(shape, lambda i: (0,) * len(shape))


def estep(base, probes, refs, table, weight):
    return pl.pallas_call(
        estep_kernel,
        grid=(GRID,),
        in_specs=[
            pl.BlockSpec(memory_space=pltpu.SMEM),
            full((NPART, WIDTH + LANES)),
            full((GROUP, PAD, CHUNK)),
            full((8, HALF)),
            full((1, HALF)),
        ],
        out_specs=[full((SHIFTS * PAD, NPART)), full((2, NPART))],
        out_shape=[
            jax.ShapeDtypeStruct((SHIFTS * PAD, NPART), f32),
            jax.ShapeDtypeStruct((2, NPART), f32),
        ],
        scratch_shapes=[
            pltpu.VMEM((GRID * PAD, WIDTH), bf16),
            pltpu.VMEM((PAD, LANES), f32),
            pltpu.VMEM((PAD, NPART), f32),
            pltpu.VMEM((8, NPART), f32),
        ],
        compiler_params=pltpu.CompilerParams(vmem_limit_bytes=48 << 20),
    )(base, probes, refs, table, weight)


def mstep_kernel(stat_ref, all_ref, p_ref, expo_ref, tab_ref, out_ref, post, sums):
    step = pl.program_id(0)
    count = all_ref.shape[0]
    peak = all_ref[0, 0:1, :]
    for d in range(1, count):
        peak = jnp.maximum(peak, all_ref[d, 0:1, :])
    mass = jnp.zeros((1, NPART), f32)
    for d in range(count):
        mass = mass + all_ref[d, 1:2, :] * jnp.exp(all_ref[d, 0:1, :] - peak)
    factor = jnp.exp(stat_ref[0:1, :] - peak) / mass
    post[...] = (expo_ref[...] * factor).astype(bf16)
    sums[...] = jnp.dot(post[...], p_ref[:, :WIDTH], preferred_element_type=f32)
    for g in range(4):
        for t in range(CHUNK // LANES):
            at = g * CHUNK + t * LANES
            lanes = slice(at, at + LANES)
            ims = slice(HALF + at, HALF + at + LANES)
            re = sums[2 * PAD : 3 * PAD, lanes]
            im = sums[2 * PAD : 3 * PAD, ims]
            for gx in (1, 2):
                c = tab_ref[2 * gx - 2 : 2 * gx - 1, lanes]
                s = tab_ref[2 * gx - 1 : 2 * gx, lanes]
                hi = slice((2 + gx) * PAD, (3 + gx) * PAD)
                lo = slice((2 - gx) * PAD, (3 - gx) * PAD)
                pr, pi = sums[hi, lanes], sums[hi, ims]
                mr, mi = sums[lo, lanes], sums[lo, ims]
                re = re + c * (pr + mr) + s * (pi - mi)
                im = im + c * (pi + mi) - s * (pr - mr)
            cy, sy = y_twiddle(tab_ref, step, lanes)
            new_re = re * cy + im * sy
            new_im = im * cy - re * sy
            chunk = slice(t * LANES, (t + 1) * LANES)

            @pl.when(step == 0)
            def _():
                out_ref[g, :, chunk] = new_re
                out_ref[g + 4, :, chunk] = new_im

            @pl.when(step > 0)
            def _():
                out_ref[g, :, chunk] += new_re
                out_ref[g + 4, :, chunk] += new_im


def mstep(stat, stats, probes, expo, table):
    return pl.pallas_call(
        mstep_kernel,
        grid=(GRID,),
        in_specs=[
            full((2, NPART)),
            full(stats.shape),
            full((NPART, WIDTH + LANES)),
            pl.BlockSpec((GRID * PAD, NPART), lambda i: (i, 0)),
            full((8, HALF)),
        ],
        out_specs=full((GROUP, PAD, CHUNK)),
        out_shape=jax.ShapeDtypeStruct((GROUP, PAD, CHUNK), f32),
        scratch_shapes=[
            pltpu.VMEM((GRID * PAD, NPART), bf16),
            pltpu.VMEM((GRID * PAD, WIDTH), f32),
        ],
        compiler_params=pltpu.CompilerParams(vmem_limit_bytes=48 << 20),
    )(stat, stats, probes, expo, table)


def per_device(images, offsets, class_lists, noise_weight, references):
    weight = noise_weight.reshape(1, HALF)
    table = jnp.asarray(twiddles())
    own = prep(images, offsets, class_lists, weight)
    probes = lax.all_gather(own, "z").reshape(NPART, WIDTH + LANES)

    mine = references.reshape(GROUP, ROWS, 48)
    mine = lax.all_to_all(mine, "z", 0, 0)
    mine = jnp.transpose(mine, (1, 0, 2)).reshape(ROWS, CHUNK)
    mine = jnp.pad(mine, ((0, PAD - ROWS), (0, 0)))
    refs = lax.all_to_all(
        jnp.broadcast_to(mine, (GROUP, PAD, CHUNK)), ("y", "xh"), 0, 0
    )

    cls = lax.axis_index("xl") * 2 + lax.axis_index("co")
    base = (cls * (ROWS * GROUP) + lax.axis_index("z") * ROWS).astype(jnp.int32).reshape(1)
    expo, stat = estep(base, probes, refs, table, weight)
    stats = lax.all_to_all(
        jnp.broadcast_to(stat, (32, 2, NPART)), ("z", "xl", "co"), 0, 0
    )
    sums = mstep(stat, stats, probes, expo, table)

    sums = jnp.sum(lax.all_to_all(sums, ("y", "xh"), 0, 0), axis=0)
    sums = jnp.transpose(sums[:ROWS].reshape(ROWS, GROUP, 48), (1, 2, 0))
    sums = lax.all_to_all(sums, "z", 0, 0)
    return jnp.transpose(sums, (1, 0, 2)).reshape(48, GROUP * ROWS)


def solution(mesh):
    fine = Mesh(mesh.devices.reshape(4, 2, 8, 2, 2), AXES)
    dom, cls = ("y", "xh", "z"), ("xl", "co")
    in_specs = (P(dom, None), P(dom, None), P(dom, None), P(), P(cls, None, dom))
    return jax.shard_map(
        per_device, mesh=fine, in_specs=in_specs, out_specs=P(dom, cls), check_vma=False
    )
```

```python
import functools
import math

import jax
import jax.numpy as jnp
import numpy as np
from jax import lax
from jax.experimental import pallas as pl
from jax.experimental.pallas import tpu as pltpu
from jax.sharding import Mesh, PartitionSpec as P

GRID = 5
BOX = 64
HALF = 1536
WIDTH = 3072
PARTS = 64
ROWS = 75
PAD = 80
LANES = 128
CHUNK = 384
GROUP = 8
NPART = PARTS * GROUP
SHIFTS = GRID * GRID
BLOCK = GRID * PAD
EXCLUDED = -1e30
SCALE = 1.0 / math.sqrt(WIDTH)
AXES = ("y", "xh", "z", "xl", "co")

f32 = jnp.float32
bf16 = jnp.bfloat16


def twiddles():
    k = np.arange(HALF)
    kx = k % BOX - BOX // 2
    ky = k // BOX
    rows = []
    for freq in (kx, ky):
        for g in (1, 2):
            angle = 2.0 * math.pi / BOX * ((g * freq) % BOX)
            rows += [np.cos(angle), np.sin(angle)]
    return np.stack(rows).astype(np.float32)


def sin_cos(turns):
    quarter = jnp.floor(turns * (1.0 / 16.0) + 0.5)
    rest = (turns - 16.0 * quarter) * (2.0 * math.pi / BOX)
    sq = rest * rest
    sin = rest * (
        1.0 + sq * (-1.0 / 6 + sq * (1.0 / 120 + sq * (-1.0 / 5040 + sq * (1.0 / 362880))))
    )
    cos = 1.0 + sq * (
        -0.5 + sq * (1.0 / 24 + sq * (-1.0 / 720 + sq * (1.0 / 40320 + sq * (-1.0 / 3628800))))
    )
    quad = quarter - 4.0 * jnp.floor(quarter * 0.25)
    swap = (quad == 1.0) | (quad == 3.0)
    sin_q = jnp.where(swap, cos, sin)
    cos_q = jnp.where(swap, sin, cos)
    sin_q = jnp.where(quad >= 2.0, -sin_q, sin_q)
    cos_q = jnp.where((quad == 1.0) | (quad == 2.0), -cos_q, cos_q)
    return sin_q, cos_q


def prep_kernel(where_ref, img_ref, offlist_ref, w_ref, out_ref, half_ref):
    eye = jnp.where(
        lax.broadcasted_iota(jnp.int32, (PARTS, PARTS), 0)
        == lax.broadcasted_iota(jnp.int32, (PARTS, PARTS), 1),
        1.0,
        0.0,
    ).astype(bf16)
    small = lax.dot_general(
        eye,
        offlist_ref[...].astype(f32).astype(bf16),
        (((1,), (1,)), ((), ())),
        preferred_element_type=f32,
    )
    ox, oy = small[:, 0:1], small[:, 1:2]
    first = where_ref[2] == 0

    def put(lanes, value):
        value = value.astype(bf16)
        out_ref[:, lanes] = value
        half_ref[:, lanes] = jnp.where(first, value[: PARTS // 2], value[PARTS // 2 :])

    for t in range(HALF // LANES):
        lanes = slice(t * LANES, (t + 1) * LANES)
        ims = slice(HALF + t * LANES, HALF + (t + 1) * LANES)
        k = lax.broadcasted_iota(jnp.int32, (1, LANES), 1) + t * LANES
        kx = ((k & (BOX - 1)) - BOX // 2).astype(f32)
        ky = (k >> 6).astype(f32)
        sin, cos = sin_cos(ox * kx + oy * ky)
        a = img_ref[:, lanes].astype(f32)
        b = img_ref[:, ims].astype(f32)
        w = w_ref[:, lanes]
        put(lanes, w * (a * cos + b * sin))
        put(ims, w * (b * cos - a * sin))
    lane = lax.broadcasted_iota(jnp.int32, (PARTS, LANES), 1).astype(f32)
    listed = small[:, 2:3] == lane
    for n in range(3, small.shape[1]):
        listed = listed | (small[:, n : n + 1] == lane)
    put(slice(WIDTH, WIDTH + LANES), jnp.where(listed, 1.0, 0.0))


def prep(where, images, offlist, weight):
    vmem = pl.BlockSpec(memory_space=pltpu.VMEM)
    return pl.pallas_call(
        prep_kernel,
        in_specs=[pl.BlockSpec(memory_space=pltpu.SMEM), vmem, vmem, vmem],
        out_shape=[
            jax.ShapeDtypeStruct((PARTS, WIDTH + LANES), bf16),
            jax.ShapeDtypeStruct((PARTS // 2, WIDTH + LANES), bf16),
        ],
    )(where, images, offlist, weight)


def y_shift(tab_ref, gy, lanes):
    row = 2 + 2 * abs(gy)
    c = tab_ref[row : row + 1, lanes]
    s = tab_ref[row + 1 : row + 2, lanes]
    return c, (s if gy > 0 else -s)


def shift_kernel(r_ref, tab_ref, w_ref, out_ref, energy_ref):
    step = pl.program_id(0)
    two = (step == 0) | (step == 4)
    zero = step == 2
    sign = jnp.where(step < 2, -1.0, 1.0)

    @pl.when(step == 0)
    def _():
        total = jnp.zeros((PAD, LANES), f32)
        for g in range(GROUP):
            for t in range(CHUNK // LANES):
                r = r_ref[g, :, t * LANES : (t + 1) * LANES].astype(f32)
                at = (g % 4) * CHUNK + t * LANES
                total = total + r * r * w_ref[:, at : at + LANES]
        energy_ref[...] = jnp.broadcast_to(
            0.5 * jnp.sum(total, axis=1, keepdims=True), energy_ref.shape
        )

    for g in range(4):
        for t in range(CHUNK // LANES):
            at = g * CHUNK + t * LANES
            lanes = slice(at, at + LANES)
            ims = slice(HALF + at, HALF + at + LANES)
            rr = r_ref[g, :, t * LANES : (t + 1) * LANES].astype(f32)
            ri = r_ref[g + 4, :, t * LANES : (t + 1) * LANES].astype(f32)
            cy = jnp.where(two, tab_ref[6:7, lanes], tab_ref[4:5, lanes])
            sy = jnp.where(two, tab_ref[7:8, lanes], tab_ref[5:6, lanes]) * sign
            cy, sy = jnp.where(zero, 1.0, cy), jnp.where(zero, 0.0, sy)
            yr = rr * cy - ri * sy
            yi = ri * cy + rr * sy
            out_ref[2 * PAD : 3 * PAD, lanes] = yr.astype(bf16)
            out_ref[2 * PAD : 3 * PAD, ims] = yi.astype(bf16)
            for gx in (1, 2):
                c = tab_ref[2 * gx - 2 : 2 * gx - 1, lanes]
                s = tab_ref[2 * gx - 1 : 2 * gx, lanes]
                cr, ci, sr, si = yr * c, yi * c, yr * s, yi * s
                hi = slice((2 + gx) * PAD, (3 + gx) * PAD)
                lo = slice((2 - gx) * PAD, (3 - gx) * PAD)
                out_ref[hi, lanes] = (cr - si).astype(bf16)
                out_ref[hi, ims] = (ci + sr).astype(bf16)
                out_ref[lo, lanes] = (cr + si).astype(bf16)
                out_ref[lo, ims] = (ci - sr).astype(bf16)


def full(shape):
    return pl.BlockSpec(shape, lambda i: (0,) * len(shape))


def shift_refs(refs, table, weight):
    return pl.pallas_call(
        shift_kernel,
        grid=(GRID,),
        in_specs=[full((GROUP, PAD, CHUNK)), full((8, HALF)), full((1, HALF))],
        out_specs=[pl.BlockSpec((BLOCK, WIDTH), lambda i: (i, 0)), full((PAD, LANES))],
        out_shape=[
            jax.ShapeDtypeStruct((SHIFTS * PAD, WIDTH), bf16),
            jax.ShapeDtypeStruct((PAD, LANES), f32),
        ],
        compiler_params=pltpu.CompilerParams(vmem_limit_bytes=32 << 20),
    )(refs, table, weight)


def block_copies(where_ref, pieces, probes, sem):
    z, co = where_ref[1], where_ref[2]
    half = PARTS // 2
    copies = []
    for n, (ref, far, mine, skip, rows) in enumerate(pieces):
        at = ((z + far + GROUP) & (GROUP - 1)) * PARTS + skip
        if mine is not None:
            at = at + half * (co if mine else 1 - co)
        at = pl.multiple_of(at, 16)
        copies.append(pltpu.make_async_copy(ref, probes.at[pl.ds(at, rows), :], sem.at[n]))
    return copies


def name_pieces(refs):
    half = PARTS // 2
    out = [(refs[0], 0, None, 0, PARTS)]
    for mine, part in ((True, refs[1:9]), (False, refs[9:17])):
        for n, far in enumerate((-1, -2, -3, 1, 2, 3)):
            out.append((part[n], far, mine, 0, half))
        out.append((part[6], 4, mine, 0, half // 2))
        out.append((part[7], 4, mine, half // 2, half // 2))
    return out


PIECES = 17


def estep_kernel(where_ref, *args):
    pieces, (shift_any, energy_ref, expo_ref, stat_ref, probes, shifted, sem, shift_sem) = (
        args[:PIECES],
        args[PIECES:],
    )
    copies = block_copies(where_ref, name_pieces(pieces), probes, sem)
    for c in copies:
        c.start()
    loads = [
        pltpu.make_async_copy(
            shift_any.at[pl.ds(b * BLOCK, BLOCK), :],
            shifted.at[pl.ds(b * BLOCK, BLOCK), :],
            shift_sem.at[b],
        )
        for b in range(GRID)
    ]
    for c in loads:
        c.start()
    row = lax.broadcasted_iota(jnp.int32, (PAD, LANES), 0)
    number = ((where_ref[0] + row) * 2731) >> 16
    lane = lax.broadcasted_iota(jnp.int32, (PAD, LANES), 1)
    pick = jnp.where((number == lane) & (row < ROWS), 1.0, 0.0).astype(bf16)
    half_energy = energy_ref[:, 0:1]
    for c in copies:
        c.wait()
    keep = (
        lax.dot_general(
            pick, probes[:, WIDTH:], (((1,), (1,)), ((), ())), preferred_element_type=f32
        )
        > 0.5
    )
    for b in range(GRID):
        loads[b].wait()
        cross = lax.dot_general(
            shifted[b * BLOCK : (b + 1) * BLOCK, :],
            probes[:, :WIDTH],
            (((1,), (1,)), ((), ())),
            preferred_element_type=f32,
        )
        best = jnp.full((8, NPART), EXCLUDED, f32)
        for gx in range(GRID):
            at = (b * GRID + gx) * PAD
            score = (cross[gx * PAD : (gx + 1) * PAD] - half_energy) * SCALE
            score = jnp.where(keep, score, EXCLUDED)
            expo_ref[at : at + PAD, :] = score
            best = jnp.maximum(best, jnp.max(score.reshape(PAD // 8, 8, NPART), axis=0))
        peak = jnp.max(best, axis=0, keepdims=True)
        mass = jnp.zeros((8, NPART), f32)
        for gx in range(GRID):
            at = (b * GRID + gx) * PAD
            e = jnp.where(keep, jnp.exp(expo_ref[at : at + PAD, :] - peak), 0.0)
            expo_ref[at : at + PAD, :] = e
            mass = mass + jnp.sum(e.reshape(PAD // 8, 8, NPART), axis=0)
        stat_ref[b : b + 1, :] = peak
        stat_ref[8 + b : 9 + b, :] = jnp.sum(mass, axis=0, keepdims=True)
    peaks = [stat_ref[b : b + 1, :] for b in range(GRID)]
    peak = functools.reduce(jnp.maximum, peaks)
    stat_ref[5:6, :] = peak
    stat_ref[6:7, :] = sum(
        stat_ref[8 + b : 9 + b, :] * jnp.exp(peaks[b] - peak) for b in range(GRID)
    )


def estep(where, pieces, shifted, energy):
    vmem = pl.BlockSpec(memory_space=pltpu.VMEM)
    anywhere = pl.BlockSpec(memory_space=pl.ANY)
    return pl.pallas_call(
        estep_kernel,
        in_specs=[pl.BlockSpec(memory_space=pltpu.SMEM)] + [anywhere] * (PIECES + 1) + [vmem],
        out_specs=[vmem, vmem],
        out_shape=[
            jax.ShapeDtypeStruct((SHIFTS * PAD, NPART), f32),
            jax.ShapeDtypeStruct((16, NPART), f32),
        ],
        scratch_shapes=[
            pltpu.VMEM((NPART, WIDTH + LANES), bf16),
            pltpu.VMEM((SHIFTS * PAD, WIDTH), bf16),
            pltpu.SemaphoreType.DMA((PIECES,)),
            pltpu.SemaphoreType.DMA((GRID,)),
        ],
        compiler_params=pltpu.CompilerParams(vmem_limit_bytes=48 << 20),
    )(where, *pieces, shifted, energy)


def mstep_kernel(where_ref, *args):
    pieces, (stat_ref, all_ref, expo_any, tab_ref, out_ref, probes, expo, sums, sem, expo_sem) = (
        args[:PIECES],
        args[PIECES:],
    )
    copies = block_copies(where_ref, name_pieces(pieces), probes, sem)
    for c in copies:
        c.start()
    loads = [
        pltpu.make_async_copy(
            expo_any.at[pl.ds(b * BLOCK, BLOCK), :],
            expo.at[pl.ds(b * BLOCK, BLOCK), :],
            expo_sem.at[b],
        )
        for b in range(GRID)
    ]
    for c in loads:
        c.start()
    count = all_ref.shape[0]
    peak = all_ref[0, 0:1, :]
    for d in range(1, count):
        peak = jnp.maximum(peak, all_ref[d, 0:1, :])
    mass = jnp.zeros((1, NPART), f32)
    for d in range(count):
        mass = mass + all_ref[d, 1:2, :] * jnp.exp(all_ref[d, 0:1, :] - peak)
    inverse = 1.0 / mass
    for c in copies:
        c.wait()
    for b in range(GRID):
        loads[b].wait()
        factor = jnp.exp(stat_ref[b : b + 1, :] - peak) * inverse
        post = (expo[b * BLOCK : (b + 1) * BLOCK, :] * factor).astype(bf16)
        sums[b % 2] = jnp.dot(post, probes[:, :WIDTH], preferred_element_type=f32)
        for g in range(4):
            for t in range(CHUNK // LANES):
                at = g * CHUNK + t * LANES
                lanes = slice(at, at + LANES)
                ims = slice(HALF + at, HALF + at + LANES)
                re = sums[b % 2, 2 * PAD : 3 * PAD, lanes]
                im = sums[b % 2, 2 * PAD : 3 * PAD, ims]
                for gx in (1, 2):
                    c = tab_ref[2 * gx - 2 : 2 * gx - 1, lanes]
                    s = tab_ref[2 * gx - 1 : 2 * gx, lanes]
                    hi = slice((2 + gx) * PAD, (3 + gx) * PAD)
                    lo = slice((2 - gx) * PAD, (3 - gx) * PAD)
                    pr, pi = sums[b % 2, hi, lanes], sums[b % 2, hi, ims]
                    mr, mi = sums[b % 2, lo, lanes], sums[b % 2, lo, ims]
                    re = re + c * (pr + mr) + s * (pi - mi)
                    im = im + c * (pi + mi) - s * (pr - mr)
                if b != 2:
                    cy, sy = y_shift(tab_ref, b - 2, lanes)
                    re, im = re * cy + im * sy, im * cy - re * sy
                chunk = slice(t * LANES, (t + 1) * LANES)
                if b == 0:
                    out_ref[g, :, chunk] = re
                    out_ref[g + 4, :, chunk] = im
                else:
                    out_ref[g, :, chunk] += re
                    out_ref[g + 4, :, chunk] += im


def mstep(where, pieces, stat, stats, expo, table):
    vmem = pl.BlockSpec(memory_space=pltpu.VMEM)
    anywhere = pl.BlockSpec(memory_space=pl.ANY)
    return pl.pallas_call(
        mstep_kernel,
        in_specs=[pl.BlockSpec(memory_space=pltpu.SMEM)]
        + [anywhere] * PIECES
        + [vmem, vmem, anywhere, vmem],
        out_specs=vmem,
        out_shape=jax.ShapeDtypeStruct((GROUP, PAD, CHUNK), f32),
        scratch_shapes=[
            pltpu.VMEM((NPART, WIDTH + LANES), bf16),
            pltpu.VMEM((SHIFTS * PAD, NPART), f32),
            pltpu.VMEM((2, BLOCK, WIDTH), f32),
            pltpu.SemaphoreType.DMA((PIECES,)),
            pltpu.SemaphoreType.DMA((GRID,)),
        ],
        compiler_params=pltpu.CompilerParams(vmem_limit_bytes=48 << 20),
    )(where, *pieces, stat, stats, expo, table)


def along_z(x, far):
    return lax.ppermute(x, "z", [(i, (i + far) % GROUP) for i in range(GROUP)])


def gather_pieces(own, half):
    up, down = [half], [half]
    for _ in range(3):
        up.append(along_z(up[-1], 1))
        down.append(along_z(down[-1], -1))
    cut = PARTS // 4
    mine = up[1:] + down[1:] + [along_z(up[-1][:cut], 1), along_z(down[-1][cut:], -1)]
    other = [lax.ppermute(x, "co", [(0, 1), (1, 0)]) for x in mine]
    return [own] + mine + other


def per_device(images, offsets, class_lists, noise_weight, references):
    weight = noise_weight.reshape(1, HALF)
    table = jnp.asarray(twiddles())
    z, co = lax.axis_index("z"), lax.axis_index("co")
    cls = lax.axis_index("xl") * 2 + co
    where = jnp.stack([cls * (ROWS * GROUP) + z * ROWS, z, co]).astype(jnp.int32)
    offlist = jnp.concatenate([offsets.T, class_lists.T], axis=0)
    own, half = prep(where, images, offlist, weight)
    pieces = gather_pieces(own, half)

    mine = references.reshape(GROUP, ROWS, 48)
    mine = lax.all_to_all(mine, "z", 0, 0)
    mine = jnp.transpose(mine, (1, 0, 2)).reshape(ROWS, CHUNK)
    mine = jnp.pad(mine, ((0, PAD - ROWS), (0, 0)))
    refs = lax.all_to_all(
        jnp.broadcast_to(mine, (GROUP, PAD, CHUNK)), ("y", "xh"), 0, 0
    )
    shifted, energy = shift_refs(refs, table, weight)

    expo, stat = estep(where, pieces, shifted, energy)
    stats = lax.all_to_all(
        jnp.broadcast_to(stat[5:7], (32, 2, NPART)), ("z", "xl", "co"), 0, 0
    )
    sums = mstep(where, pieces, stat, stats, expo, table)

    sums = jnp.sum(lax.all_to_all(sums, ("y", "xh"), 0, 0), axis=0)
    sums = jnp.transpose(sums[:ROWS].reshape(ROWS, GROUP, 48), (1, 2, 0))
    sums = lax.all_to_all(sums, "z", 0, 0)
    return jnp.transpose(sums, (1, 0, 2)).reshape(48, GROUP * ROWS)


def solution(mesh):
    fine = Mesh(mesh.devices.reshape(4, 2, 8, 2, 2), AXES)
    dom, cls = ("y", "xh", "z"), ("xl", "co")
    in_specs = (P(dom, None), P(dom, None), P(dom, None), P(), P(cls, None, dom))
    return jax.shard_map(
        per_device, mesh=fine, in_specs=in_specs, out_specs=P(dom, cls), check_vma=False
    )
```

```python
import functools
import math

import jax
import jax.numpy as jnp
from jax import lax
from jax.experimental import pallas as pl
from jax.experimental.pallas import tpu as pltpu
from jax.sharding import Mesh, PartitionSpec as P

GRID = 5
BOX = 64
HALF = 1536
WIDTH = 3072
PARTS = 64
ROWS = 75
PAD = 80
LANES = 128
CHUNK = 384
GROUP = 8
NPART = PARTS * GROUP
SHIFTS = GRID * GRID
BLOCK = GRID * PAD
EXCLUDED = -1e30
SCALE = 1.0 / math.sqrt(WIDTH)
AXES = ("y", "xh", "z", "xl", "co")

f32 = jnp.float32
bf16 = jnp.bfloat16


def sin_cos(turns):
    quarter = jnp.floor(turns * (1.0 / 16.0) + 0.5)
    rest = (turns - 16.0 * quarter) * (2.0 * math.pi / BOX)
    sq = rest * rest
    sin = rest * (
        1.0 + sq * (-1.0 / 6 + sq * (1.0 / 120 + sq * (-1.0 / 5040 + sq * (1.0 / 362880))))
    )
    cos = 1.0 + sq * (
        -0.5 + sq * (1.0 / 24 + sq * (-1.0 / 720 + sq * (1.0 / 40320 + sq * (-1.0 / 3628800))))
    )
    quad = quarter - 4.0 * jnp.floor(quarter * 0.25)
    swap = (quad == 1.0) | (quad == 3.0)
    sin_q = jnp.where(swap, cos, sin)
    cos_q = jnp.where(swap, sin, cos)
    sin_q = jnp.where(quad >= 2.0, -sin_q, sin_q)
    cos_q = jnp.where((quad == 1.0) | (quad == 2.0), -cos_q, cos_q)
    return sin_q, cos_q


def prep_kernel(img_ref, off_ref, list_ref, w_ref, out_ref, half_ref, tab_ref):
    eye = jnp.where(
        lax.broadcasted_iota(jnp.int32, (PARTS, PARTS), 0)
        == lax.broadcasted_iota(jnp.int32, (PARTS, PARTS), 1),
        1.0,
        0.0,
    ).astype(bf16)

    def upright(ref):
        flat = ref[...].astype(f32).astype(bf16)
        return lax.dot_general(eye, flat, (((1,), (1,)), ((), ())), preferred_element_type=f32)

    off = upright(off_ref)
    ox, oy = off[:, 0:1], off[:, 1:2]
    first = lax.axis_index("co") == 0

    def put(lanes, value):
        value = value.astype(bf16)
        out_ref[:, lanes] = value
        half_ref[:, lanes] = jnp.where(first, value[: PARTS // 2], value[PARTS // 2 :])

    for t in range(HALF // LANES):
        lanes = slice(t * LANES, (t + 1) * LANES)
        ims = slice(HALF + t * LANES, HALF + (t + 1) * LANES)
        k = lax.broadcasted_iota(jnp.int32, (1, LANES), 1) + t * LANES
        kx = ((k & (BOX - 1)) - BOX // 2).astype(f32)
        ky = (k >> 6).astype(f32)
        sin, cos = sin_cos(ox * kx + oy * ky)
        a = img_ref[:, lanes].astype(f32)
        b = img_ref[:, ims].astype(f32)
        w = w_ref[lanes].reshape(1, LANES)
        put(lanes, w * (a * cos + b * sin))
        put(ims, w * (b * cos - a * sin))
        step = lax.broadcasted_iota(jnp.int32, (8, 1), 0)
        move = (((step >> 1) & 1) + 1).astype(f32)
        freq = jnp.where(step < 4, kx, ky)
        tab_sin, tab_cos = sin_cos(move * freq)
        tab_ref[0:8, lanes] = jnp.where((step & 1) == 0, tab_cos, tab_sin)
        tab_ref[8:16, lanes] = jnp.broadcast_to(w, (8, LANES))
    lists = upright(list_ref)
    lane = lax.broadcasted_iota(jnp.int32, (PARTS, LANES), 1).astype(f32)
    listed = lists[:, 0:1] == lane
    for n in range(1, lists.shape[1]):
        listed = listed | (lists[:, n : n + 1] == lane)
    put(slice(WIDTH, WIDTH + LANES), jnp.where(listed, 1.0, 0.0))


VMEM = pl.BlockSpec(memory_space=pltpu.VMEM)
ANYWHERE = pl.BlockSpec(memory_space=pl.ANY)


def prep(images, offsets, class_lists, weight):
    return pl.pallas_call(
        prep_kernel,
        in_specs=[VMEM] * 4,
        out_specs=[VMEM] * 3,
        out_shape=[
            jax.ShapeDtypeStruct((PARTS, WIDTH + LANES), bf16),
            jax.ShapeDtypeStruct((PARTS // 2, WIDTH + LANES), bf16),
            jax.ShapeDtypeStruct((16, HALF), f32),
        ],
        compiler_params=pltpu.CompilerParams(vmem_limit_bytes=4 << 20),
    )(images, offsets, class_lists, weight)


def y_shift(tab_ref, gy, lanes):
    row = 2 + 2 * abs(gy)
    c = tab_ref[row : row + 1, lanes]
    s = tab_ref[row + 1 : row + 2, lanes]
    return c, (s if gy > 0 else -s)


def shift_kernel(r_ref, tab_ref, out_ref, energy_ref, total):
    total[...] = jnp.zeros_like(total)

    def chunk(n, carry):
        at = pl.multiple_of(n * LANES, LANES)
        lanes, ims = pl.ds(at, LANES), pl.ds(HALF + at, LANES)
        rr = r_ref[lanes, :].astype(f32).T[:PAD]
        ri = r_ref[ims, :].astype(f32).T[:PAD]
        total[...] += (rr * rr + ri * ri) * tab_ref[8:9, lanes]
        for gy in range(-2, 3):
            yr, yi = rr, ri
            if gy:
                c, s = y_shift(tab_ref, gy, lanes)
                yr, yi = rr * c - ri * s, ri * c + rr * s
            mid = ((gy + 2) * GRID + 2) * PAD
            out_ref[mid : mid + PAD, lanes] = yr.astype(bf16)
            out_ref[mid : mid + PAD, ims] = yi.astype(bf16)
            for gx in (1, 2):
                c = tab_ref[2 * gx - 2 : 2 * gx - 1, lanes]
                s = tab_ref[2 * gx - 1 : 2 * gx, lanes]
                cr, ci, sr, si = yr * c, yi * c, yr * s, yi * s
                hi = slice(mid + gx * PAD, mid + (gx + 1) * PAD)
                lo = slice(mid - gx * PAD, mid - (gx - 1) * PAD)
                out_ref[hi, lanes] = (cr - si).astype(bf16)
                out_ref[hi, ims] = (ci + sr).astype(bf16)
                out_ref[lo, lanes] = (cr + si).astype(bf16)
                out_ref[lo, ims] = (ci - sr).astype(bf16)
        return carry

    lax.fori_loop(0, HALF // LANES, chunk, 0)
    energy_ref[...] = jnp.broadcast_to(
        0.5 * jnp.sum(total[...], axis=1, keepdims=True), energy_ref.shape
    )


def shift_refs(refs, table):
    return pl.pallas_call(
        shift_kernel,
        in_specs=[VMEM] * 2,
        out_specs=[VMEM] * 2,
        out_shape=[
            jax.ShapeDtypeStruct((SHIFTS * PAD, WIDTH), bf16),
            jax.ShapeDtypeStruct((PAD, LANES), f32),
        ],
        scratch_shapes=[pltpu.VMEM((PAD, LANES), f32)],
        compiler_params=pltpu.CompilerParams(vmem_limit_bytes=16 << 20),
    )(refs, table)


def block_copies(pieces, probes, sem):
    z, co = lax.axis_index("z"), lax.axis_index("co")
    half = PARTS // 2
    copies = []
    for n, (ref, far, mine, skip, rows) in enumerate(pieces):
        at = ((z + far + GROUP) & (GROUP - 1)) * PARTS + skip
        if mine is not None:
            at = at + half * (co if mine else 1 - co)
        at = pl.multiple_of(at, 16)
        copies.append(pltpu.make_async_copy(ref, probes.at[pl.ds(at, rows), :], sem.at[n]))
    return copies


def name_pieces(refs):
    half = PARTS // 2
    out = [(refs[0], 0, None, 0, PARTS)]
    for mine, part in ((True, refs[1:9]), (False, refs[9:17])):
        for n, far in enumerate((-1, -2, -3, 1, 2, 3)):
            out.append((part[n], far, mine, 0, half))
        out.append((part[6], 4, mine, 0, half // 2))
        out.append((part[7], 4, mine, half // 2, half // 2))
    return out


PIECES = 17


def estep_kernel(*args):
    pieces, (shifted, energy_ref, probes, expo_ref, stat_ref, sem) = args[:PIECES], args[PIECES:]
    copies = block_copies(name_pieces(pieces), probes, sem)
    for c in copies:
        c.start()
    cls = lax.axis_index("xl") * 2 + lax.axis_index("co")
    base = cls * (ROWS * GROUP) + lax.axis_index("z") * ROWS
    row = lax.broadcasted_iota(jnp.int32, (PAD, LANES), 0)
    number = ((base + row) * 2731) >> 16
    lane = lax.broadcasted_iota(jnp.int32, (PAD, LANES), 1)
    pick = jnp.where((number == lane) & (row < ROWS), 1.0, 0.0).astype(bf16)
    half_energy = energy_ref[:, 0:1]
    for c in copies:
        c.wait()
    keep = (
        lax.dot_general(
            pick, probes[:, WIDTH:], (((1,), (1,)), ((), ())), preferred_element_type=f32
        )
        > 0.5
    )
    for b in range(GRID):
        cross = lax.dot_general(
            shifted[b * BLOCK : (b + 1) * BLOCK, :],
            probes[:, :WIDTH],
            (((1,), (1,)), ((), ())),
            preferred_element_type=f32,
        )
        best = jnp.full((8, NPART), EXCLUDED, f32)
        for gx in range(GRID):
            at = (b * GRID + gx) * PAD
            score = (cross[gx * PAD : (gx + 1) * PAD] - half_energy) * SCALE
            score = jnp.where(keep, score, EXCLUDED)
            expo_ref[at : at + PAD, :] = score
            best = jnp.maximum(best, jnp.max(score.reshape(PAD // 8, 8, NPART), axis=0))
        peak = jnp.max(best, axis=0, keepdims=True)
        mass = jnp.zeros((8, NPART), f32)
        for gx in range(GRID):
            at = (b * GRID + gx) * PAD
            e = jnp.where(keep, jnp.exp(expo_ref[at : at + PAD, :] - peak), 0.0)
            expo_ref[at : at + PAD, :] = e
            mass = mass + jnp.sum(e.reshape(PAD // 8, 8, NPART), axis=0)
        stat_ref[b : b + 1, :] = peak
        stat_ref[8 + b : 9 + b, :] = jnp.sum(mass, axis=0, keepdims=True)
    peaks = [stat_ref[b : b + 1, :] for b in range(GRID)]
    peak = functools.reduce(jnp.maximum, peaks)
    stat_ref[5:6, :] = peak
    stat_ref[6:7, :] = sum(
        stat_ref[8 + b : 9 + b, :] * jnp.exp(peaks[b] - peak) for b in range(GRID)
    )


def estep(pieces, shifted, energy):
    return pl.pallas_call(
        estep_kernel,
        in_specs=[ANYWHERE] * PIECES + [VMEM] * 2,
        out_specs=[VMEM] * 3,
        out_shape=[
            jax.ShapeDtypeStruct((NPART, WIDTH + LANES), bf16),
            jax.ShapeDtypeStruct((SHIFTS * PAD, NPART), f32),
            jax.ShapeDtypeStruct((16, NPART), f32),
        ],
        scratch_shapes=[pltpu.SemaphoreType.DMA((PIECES,))],
        compiler_params=pltpu.CompilerParams(vmem_limit_bytes=26 << 20),
    )(*pieces, shifted, energy)


STRIP = 256


def mstep_kernel(stat_ref, all_ref, p_ref, expo_ref, tab_ref, out_ref, post, sums):
    count = all_ref.shape[0]
    peak = all_ref[0, 0:1, :]
    for d in range(1, count):
        peak = jnp.maximum(peak, all_ref[d, 0:1, :])
    mass = jnp.zeros((1, NPART), f32)
    for d in range(count):
        mass = mass + all_ref[d, 1:2, :] * jnp.exp(all_ref[d, 0:1, :] - peak)
    inverse = 1.0 / mass
    for b in range(GRID):
        rows = slice(b * BLOCK, (b + 1) * BLOCK)
        factor = jnp.exp(stat_ref[b : b + 1, :] - peak) * inverse
        post[rows, :] = (expo_ref[rows, :] * factor).astype(bf16)
    turn = 0
    for strip in range(HALF // STRIP):
        re_cols = slice(strip * STRIP, (strip + 1) * STRIP)
        im_cols = slice(HALF + strip * STRIP, HALF + (strip + 1) * STRIP)
        for b in range(GRID):
            rows = slice(b * BLOCK, (b + 1) * BLOCK)
            k = turn % 2
            turn += 1
            sums[k, :, :STRIP] = jnp.dot(
                post[rows, :], p_ref[:, re_cols], preferred_element_type=f32
            )
            sums[k, :, STRIP:] = jnp.dot(
                post[rows, :], p_ref[:, im_cols], preferred_element_type=f32
            )
            for t in range(STRIP // LANES):
                at = strip * STRIP + t * LANES
                lanes = slice(at, at + LANES)
                res = slice(t * LANES, (t + 1) * LANES)
                ims = slice(STRIP + t * LANES, STRIP + (t + 1) * LANES)
                re = sums[k, 2 * PAD : 3 * PAD, res]
                im = sums[k, 2 * PAD : 3 * PAD, ims]
                for gx in (1, 2):
                    c = tab_ref[2 * gx - 2 : 2 * gx - 1, lanes]
                    s = tab_ref[2 * gx - 1 : 2 * gx, lanes]
                    hi = slice((2 + gx) * PAD, (3 + gx) * PAD)
                    lo = slice((2 - gx) * PAD, (3 - gx) * PAD)
                    pr, pi = sums[k, hi, res], sums[k, hi, ims]
                    mr, mi = sums[k, lo, res], sums[k, lo, ims]
                    re = re + c * (pr + mr) + s * (pi - mi)
                    im = im + c * (pi + mi) - s * (pr - mr)
                if b != 2:
                    cy, sy = y_shift(tab_ref, b - 2, lanes)
                    re, im = re * cy + im * sy, im * cy - re * sy
                g, chunk = at // CHUNK, slice(at % CHUNK, at % CHUNK + LANES)
                if b == 0:
                    out_ref[g, :, chunk] = re
                    out_ref[g + 4, :, chunk] = im
                else:
                    out_ref[g, :, chunk] += re
                    out_ref[g + 4, :, chunk] += im


def mstep(stat, stats, probes, expo, table):
    return pl.pallas_call(
        mstep_kernel,
        in_specs=[VMEM] * 5,
        out_specs=VMEM,
        out_shape=jax.ShapeDtypeStruct((GROUP, PAD, CHUNK), f32),
        scratch_shapes=[
            pltpu.VMEM((SHIFTS * PAD, NPART), bf16),
            pltpu.VMEM((2, BLOCK, 2 * STRIP), f32),
        ],
        compiler_params=pltpu.CompilerParams(vmem_limit_bytes=20 << 20),
    )(stat, stats, probes, expo, table)


def along_z(x, far):
    return lax.ppermute(x, "z", [(i, (i + far) % GROUP) for i in range(GROUP)])


def gather_pieces(own, half):
    up, down = [half], [half]
    for _ in range(3):
        up.append(along_z(up[-1], 1))
        down.append(along_z(down[-1], -1))
    cut = PARTS // 4
    mine = up[1:] + down[1:] + [along_z(up[-1][:cut], 1), along_z(down[-1][cut:], -1)]
    other = [lax.ppermute(x, "co", [(0, 1), (1, 0)]) for x in mine]
    return [own] + mine + other


def per_device(images, offsets, class_lists, noise_weight, references):
    mine = references.reshape(GROUP, ROWS, 48)
    mine = jnp.pad(jnp.transpose(mine, (0, 2, 1)), ((0, 0), (0, 0), (0, PAD - ROWS)))
    mine = jnp.broadcast_to(mine[None], (GROUP, GROUP, 48, PAD)).reshape(-1, 48, PAD)
    refs = lax.all_to_all(mine, ("y", "xh", "z"), 0, 0).reshape(WIDTH, PAD)

    own, half, table = prep(images, offsets.T, class_lists.T, noise_weight)
    pieces = gather_pieces(own, half)
    shifted, energy = shift_refs(refs, table)

    probes, expo, stat = estep(pieces, shifted, energy)
    stats = lax.all_to_all(
        jnp.broadcast_to(stat[5:7], (32, 2, NPART)), ("z", "xl", "co"), 0, 0
    )
    sums = mstep(stat, stats, probes, expo, table)

    sums = jnp.sum(lax.all_to_all(sums, ("y", "xh"), 0, 0), axis=0)
    sums = jnp.transpose(sums[:ROWS].reshape(ROWS, GROUP, 48), (1, 2, 0))
    sums = lax.all_to_all(sums, "z", 0, 0)
    return jnp.transpose(sums, (1, 0, 2)).reshape(48, GROUP * ROWS)


def solution(mesh):
    fine = Mesh(mesh.devices.reshape(4, 2, 8, 2, 2), AXES)
    dom, cls = ("y", "xh", "z"), ("xl", "co")
    in_specs = (P(dom, None), P(dom, None), P(dom, None), P(), P(cls, None, dom))
    return jax.shard_map(
        per_device, mesh=fine, in_specs=in_specs, out_specs=P(dom, cls), check_vma=False
    )
```

```python
import functools
import math

import jax
import jax.numpy as jnp
from jax import lax
from jax.experimental import pallas as pl
from jax.experimental.pallas import tpu as pltpu
from jax.sharding import Mesh, PartitionSpec as P

GRID = 5
BOX = 64
HALF = 1536
WIDTH = 3072
PARTS = 64
ROWS = 75
PAD = 80
LANES = 128
CHUNK = 384
GROUP = 8
NPART = PARTS * GROUP
SHIFTS = GRID * GRID
BLOCK = GRID * PAD
EXCLUDED = -1e30
SCALE = 1.0 / math.sqrt(WIDTH)
AXES = ("y", "xh", "z", "xl", "co")

f32 = jnp.float32
bf16 = jnp.bfloat16


def sin_cos(turns):
    quarter = jnp.floor(turns * (1.0 / 16.0) + 0.5)
    rest = (turns - 16.0 * quarter) * (2.0 * math.pi / BOX)
    sq = rest * rest
    sin = rest * (
        1.0 + sq * (-1.0 / 6 + sq * (1.0 / 120 + sq * (-1.0 / 5040 + sq * (1.0 / 362880))))
    )
    cos = 1.0 + sq * (
        -0.5 + sq * (1.0 / 24 + sq * (-1.0 / 720 + sq * (1.0 / 40320 + sq * (-1.0 / 3628800))))
    )
    quad = quarter - 4.0 * jnp.floor(quarter * 0.25)
    swap = (quad == 1.0) | (quad == 3.0)
    sin_q = jnp.where(swap, cos, sin)
    cos_q = jnp.where(swap, sin, cos)
    sin_q = jnp.where(quad >= 2.0, -sin_q, sin_q)
    cos_q = jnp.where((quad == 1.0) | (quad == 2.0), -cos_q, cos_q)
    return sin_q, cos_q


def prep_kernel(img_ref, off_ref, list_ref, w_ref, out_ref, half_ref, tab_ref):
    eye = jnp.where(
        lax.broadcasted_iota(jnp.int32, (PARTS, PARTS), 0)
        == lax.broadcasted_iota(jnp.int32, (PARTS, PARTS), 1),
        1.0,
        0.0,
    ).astype(bf16)

    def upright(ref):
        flat = ref[...].astype(f32).astype(bf16)
        return lax.dot_general(eye, flat, (((1,), (1,)), ((), ())), preferred_element_type=f32)

    off = upright(off_ref)
    ox, oy = off[:, 0:1], off[:, 1:2]
    first = lax.axis_index("co") == 0

    def put(lanes, value):
        value = value.astype(bf16)
        out_ref[:, lanes] = value
        half_ref[:, lanes] = jnp.where(first, value[: PARTS // 2], value[PARTS // 2 :])

    for t in range(HALF // LANES):
        lanes = slice(t * LANES, (t + 1) * LANES)
        ims = slice(HALF + t * LANES, HALF + (t + 1) * LANES)
        k = lax.broadcasted_iota(jnp.int32, (1, LANES), 1) + t * LANES
        kx = ((k & (BOX - 1)) - BOX // 2).astype(f32)
        ky = (k >> 6).astype(f32)
        sin, cos = sin_cos(ox * kx + oy * ky)
        a = img_ref[:, lanes].astype(f32)
        b = img_ref[:, ims].astype(f32)
        w = w_ref[lanes].reshape(1, LANES)
        put(lanes, w * (a * cos + b * sin))
        put(ims, w * (b * cos - a * sin))
        step = lax.broadcasted_iota(jnp.int32, (8, 1), 0)
        move = (((step >> 1) & 1) + 1).astype(f32)
        freq = jnp.where(step < 4, kx, ky)
        tab_sin, tab_cos = sin_cos(move * freq)
        tab_ref[0:8, lanes] = jnp.where((step & 1) == 0, tab_cos, tab_sin)
        tab_ref[8:16, lanes] = jnp.broadcast_to(w, (8, LANES))
    lists = upright(list_ref)
    lane = lax.broadcasted_iota(jnp.int32, (PARTS, LANES), 1).astype(f32)
    listed = lists[:, 0:1] == lane
    for n in range(1, lists.shape[1]):
        listed = listed | (lists[:, n : n + 1] == lane)
    put(slice(WIDTH, WIDTH + LANES), jnp.where(listed, 1.0, 0.0))


VMEM = pl.BlockSpec(memory_space=pltpu.VMEM)


def prep(images, offsets, class_lists, weight):
    return pl.pallas_call(
        prep_kernel,
        in_specs=[VMEM] * 4,
        out_specs=[VMEM] * 3,
        out_shape=[
            jax.ShapeDtypeStruct((PARTS, WIDTH + LANES), bf16),
            jax.ShapeDtypeStruct((PARTS // 2, WIDTH + LANES), bf16),
            jax.ShapeDtypeStruct((16, HALF), f32),
        ],
        cost_estimate=pl.CostEstimate(flops=4 << 20, bytes_accessed=1 << 20, transcendentals=0),
    )(images, offsets, class_lists, weight)


def y_shift(tab_ref, gy, lanes):
    row = 2 + 2 * abs(gy)
    c = tab_ref[row : row + 1, lanes]
    s = tab_ref[row + 1 : row + 2, lanes]
    return c, (s if gy > 0 else -s)


def shift_kernel(r_ref, tab_ref, out_ref, energy_ref, total):
    total[...] = jnp.zeros_like(total)

    def chunk(n, carry):
        at = pl.multiple_of(n * LANES, LANES)
        lanes, ims = pl.ds(at, LANES), pl.ds(HALF + at, LANES)
        rr = r_ref[lanes, :].astype(f32).T[:PAD]
        ri = r_ref[ims, :].astype(f32).T[:PAD]
        total[...] += (rr * rr + ri * ri) * tab_ref[8:9, lanes]
        for gy in range(-2, 3):
            yr, yi = rr, ri
            if gy:
                c, s = y_shift(tab_ref, gy, lanes)
                yr, yi = rr * c - ri * s, ri * c + rr * s
            mid = ((gy + 2) * GRID + 2) * PAD
            out_ref[mid : mid + PAD, lanes] = yr.astype(bf16)
            out_ref[mid : mid + PAD, ims] = yi.astype(bf16)
            for gx in (1, 2):
                c = tab_ref[2 * gx - 2 : 2 * gx - 1, lanes]
                s = tab_ref[2 * gx - 1 : 2 * gx, lanes]
                cr, ci, sr, si = yr * c, yi * c, yr * s, yi * s
                hi = slice(mid + gx * PAD, mid + (gx + 1) * PAD)
                lo = slice(mid - gx * PAD, mid - (gx - 1) * PAD)
                out_ref[hi, lanes] = (cr - si).astype(bf16)
                out_ref[hi, ims] = (ci + sr).astype(bf16)
                out_ref[lo, lanes] = (cr + si).astype(bf16)
                out_ref[lo, ims] = (ci - sr).astype(bf16)
        return carry

    lax.fori_loop(0, HALF // LANES, chunk, 0)
    energy_ref[...] = jnp.broadcast_to(
        0.5 * jnp.sum(total[...], axis=1, keepdims=True), energy_ref.shape
    )


def shift_refs(refs, table):
    return pl.pallas_call(
        shift_kernel,
        in_specs=[VMEM] * 2,
        out_specs=[VMEM] * 2,
        out_shape=[
            jax.ShapeDtypeStruct((SHIFTS * PAD, WIDTH), bf16),
            jax.ShapeDtypeStruct((PAD, LANES), f32),
        ],
        scratch_shapes=[pltpu.VMEM((PAD, LANES), f32)],
        compiler_params=pltpu.CompilerParams(vmem_limit_bytes=16 << 20),
        cost_estimate=pl.CostEstimate(flops=40 << 20, bytes_accessed=14 << 20, transcendentals=0),
    )(refs, table)


def assemble(pieces, probes):
    z, co = lax.axis_index("z"), lax.axis_index("co")
    half = PARTS // 2
    for ref, far, mine, skip, rows in pieces:
        at = ((z + far + GROUP) & (GROUP - 1)) * PARTS + skip
        if mine is not None:
            at = at + half * (co if mine else 1 - co)
        probes[pl.ds(pl.multiple_of(at, 16), rows), :] = ref[...]


def name_pieces(refs):
    half = PARTS // 2
    out = [(refs[0], 0, None, 0, PARTS)]
    for mine, part in ((True, refs[1:9]), (False, refs[9:17])):
        for n, far in enumerate((-1, -2, -3, 1, 2, 3)):
            out.append((part[n], far, mine, 0, half))
        out.append((part[6], 4, mine, 0, half // 2))
        out.append((part[7], 4, mine, half // 2, half // 2))
    return out


PIECES = 17


def estep_kernel(*args):
    pieces, (shifted, energy_ref, probes, expo_ref, stat_ref) = args[:PIECES], args[PIECES:]
    assemble(name_pieces(pieces), probes)
    cls = lax.axis_index("xl") * 2 + lax.axis_index("co")
    base = cls * (ROWS * GROUP) + lax.axis_index("z") * ROWS
    row = lax.broadcasted_iota(jnp.int32, (PAD, LANES), 0)
    number = ((base + row) * 2731) >> 16
    lane = lax.broadcasted_iota(jnp.int32, (PAD, LANES), 1)
    pick = jnp.where((number == lane) & (row < ROWS), 1.0, 0.0).astype(bf16)
    half_energy = energy_ref[:, 0:1]
    keep = (
        lax.dot_general(
            pick, probes[:, WIDTH:], (((1,), (1,)), ((), ())), preferred_element_type=f32
        )
        > 0.5
    )
    for b in range(GRID):
        cross = lax.dot_general(
            shifted[b * BLOCK : (b + 1) * BLOCK, :],
            probes[:, :WIDTH],
            (((1,), (1,)), ((), ())),
            preferred_element_type=f32,
        )
        best = jnp.full((8, NPART), EXCLUDED, f32)
        for gx in range(GRID):
            at = (b * GRID + gx) * PAD
            score = (cross[gx * PAD : (gx + 1) * PAD] - half_energy) * SCALE
            score = jnp.where(keep, score, EXCLUDED)
            expo_ref[at : at + PAD, :] = score
            best = jnp.maximum(best, jnp.max(score.reshape(PAD // 8, 8, NPART), axis=0))
        peak = jnp.max(best, axis=0, keepdims=True)
        mass = jnp.zeros((8, NPART), f32)
        for gx in range(GRID):
            at = (b * GRID + gx) * PAD
            e = jnp.where(keep, jnp.exp(expo_ref[at : at + PAD, :] - peak), 0.0)
            expo_ref[at : at + PAD, :] = e
            mass = mass + jnp.sum(e.reshape(PAD // 8, 8, NPART), axis=0)
        stat_ref[b : b + 1, :] = peak
        stat_ref[8 + b : 9 + b, :] = jnp.sum(mass, axis=0, keepdims=True)
    peaks = [stat_ref[b : b + 1, :] for b in range(GRID)]
    peak = functools.reduce(jnp.maximum, peaks)
    stat_ref[5:6, :] = peak
    stat_ref[6:7, :] = sum(
        stat_ref[8 + b : 9 + b, :] * jnp.exp(peaks[b] - peak) for b in range(GRID)
    )


def estep(pieces, shifted, energy):
    return pl.pallas_call(
        estep_kernel,
        in_specs=[VMEM] * (PIECES + 2),
        out_specs=[VMEM] * 3,
        out_shape=[
            jax.ShapeDtypeStruct((NPART, WIDTH + LANES), bf16),
            jax.ShapeDtypeStruct((SHIFTS * PAD, NPART), f32),
            jax.ShapeDtypeStruct((16, NPART), f32),
        ],
        compiler_params=pltpu.CompilerParams(vmem_limit_bytes=30 << 20),
        cost_estimate=pl.CostEstimate(
            flops=2 * SHIFTS * PAD * NPART * WIDTH,
            bytes_accessed=24 << 20,
            transcendentals=SHIFTS * PAD * NPART,
        ),
    )(*pieces, shifted, energy)


STRIP = 256


def mstep_kernel(stat_ref, all_ref, p_ref, expo_ref, tab_ref, out_ref, post, sums):
    count = all_ref.shape[0]
    peak = all_ref[0, 0:1, :]
    for d in range(1, count):
        peak = jnp.maximum(peak, all_ref[d, 0:1, :])
    mass = jnp.zeros((1, NPART), f32)
    for d in range(count):
        mass = mass + all_ref[d, 1:2, :] * jnp.exp(all_ref[d, 0:1, :] - peak)
    inverse = 1.0 / mass
    for b in range(GRID):
        rows = slice(b * BLOCK, (b + 1) * BLOCK)
        factor = jnp.exp(stat_ref[b : b + 1, :] - peak) * inverse
        post[rows, :] = (expo_ref[rows, :] * factor).astype(bf16)
    turn = 0
    for strip in range(HALF // STRIP):
        re_cols = slice(strip * STRIP, (strip + 1) * STRIP)
        im_cols = slice(HALF + strip * STRIP, HALF + (strip + 1) * STRIP)
        for b in range(GRID):
            rows = slice(b * BLOCK, (b + 1) * BLOCK)
            k = turn % 2
            turn += 1
            sums[k, :, :STRIP] = jnp.dot(
                post[rows, :], p_ref[:, re_cols], preferred_element_type=f32
            )
            sums[k, :, STRIP:] = jnp.dot(
                post[rows, :], p_ref[:, im_cols], preferred_element_type=f32
            )
            for t in range(STRIP // LANES):
                at = strip * STRIP + t * LANES
                lanes = slice(at, at + LANES)
                res = slice(t * LANES, (t + 1) * LANES)
                ims = slice(STRIP + t * LANES, STRIP + (t + 1) * LANES)
                re = sums[k, 2 * PAD : 3 * PAD, res]
                im = sums[k, 2 * PAD : 3 * PAD, ims]
                for gx in (1, 2):
                    c = tab_ref[2 * gx - 2 : 2 * gx - 1, lanes]
                    s = tab_ref[2 * gx - 1 : 2 * gx, lanes]
                    hi = slice((2 + gx) * PAD, (3 + gx) * PAD)
                    lo = slice((2 - gx) * PAD, (3 - gx) * PAD)
                    pr, pi = sums[k, hi, res], sums[k, hi, ims]
                    mr, mi = sums[k, lo, res], sums[k, lo, ims]
                    re = re + c * (pr + mr) + s * (pi - mi)
                    im = im + c * (pi + mi) - s * (pr - mr)
                if b != 2:
                    cy, sy = y_shift(tab_ref, b - 2, lanes)
                    re, im = re * cy + im * sy, im * cy - re * sy
                g, chunk = at // CHUNK, slice(at % CHUNK, at % CHUNK + LANES)
                if b == 0:
                    out_ref[g, :, chunk] = re
                    out_ref[g + 4, :, chunk] = im
                else:
                    out_ref[g, :, chunk] += re
                    out_ref[g + 4, :, chunk] += im


def mstep(stat, stats, probes, expo, table):
    return pl.pallas_call(
        mstep_kernel,
        in_specs=[VMEM] * 5,
        out_specs=VMEM,
        out_shape=jax.ShapeDtypeStruct((GROUP, PAD, CHUNK), f32),
        scratch_shapes=[
            pltpu.VMEM((SHIFTS * PAD, NPART), bf16),
            pltpu.VMEM((2, BLOCK, 2 * STRIP), f32),
        ],
        compiler_params=pltpu.CompilerParams(vmem_limit_bytes=20 << 20),
        cost_estimate=pl.CostEstimate(
            flops=2 * SHIFTS * PAD * NPART * WIDTH, bytes_accessed=9 << 20, transcendentals=0
        ),
    )(stat, stats, probes, expo, table)


def along_z(x, far):
    return lax.ppermute(x, "z", [(i, (i + far) % GROUP) for i in range(GROUP)])


def gather_pieces(own, half):
    up, down = [half], [half]
    for _ in range(3):
        up.append(along_z(up[-1], 1))
        down.append(along_z(down[-1], -1))
    cut = PARTS // 4
    mine = up[1:] + down[1:] + [along_z(up[-1][:cut], 1), along_z(down[-1][cut:], -1)]
    other = [lax.ppermute(x, "co", [(0, 1), (1, 0)]) for x in mine]
    return [own] + mine + other


def per_device(images, offsets, class_lists, noise_weight, references):
    mine = references.reshape(GROUP, ROWS, 48)
    mine = jnp.pad(jnp.transpose(mine, (0, 2, 1)), ((0, 0), (0, 0), (0, LANES - ROWS)))
    mine = lax.all_to_all(mine, "z", 0, 0).reshape(CHUNK, LANES)
    mine = jnp.broadcast_to(mine, (GROUP, CHUNK, LANES))
    refs = lax.all_to_all(mine, ("y", "xh"), 0, 0).reshape(WIDTH, LANES)

    own, half, table = prep(images, offsets.T, class_lists.T, noise_weight)
    pieces = gather_pieces(own, half)
    shifted, energy = shift_refs(refs, table)

    probes, expo, stat = estep(pieces, shifted, energy)
    stats = lax.all_to_all(
        jnp.broadcast_to(stat[5:7], (32, 2, NPART)), ("z", "xl", "co"), 0, 0
    )
    sums = mstep(stat, stats, probes, expo, table)

    sums = jnp.sum(lax.all_to_all(sums, ("y", "xh"), 0, 0), axis=0)
    sums = jnp.pad(sums.T, ((0, 0), (0, LANES - PAD))).reshape(GROUP, 48, LANES)
    sums = lax.all_to_all(sums, "z", 0, 0)[:, :, :ROWS]
    return jnp.transpose(sums, (1, 0, 2)).reshape(48, GROUP * ROWS)


def solution(mesh):
    fine = Mesh(mesh.devices.reshape(4, 2, 8, 2, 2), AXES)
    dom, cls = ("y", "xh", "z"), ("xl", "co")
    in_specs = (P(dom, None), P(dom, None), P(dom, None), P(), P(cls, None, dom))
    return jax.shard_map(
        per_device, mesh=fine, in_specs=in_specs, out_specs=P(dom, cls), check_vma=False
    )
```

```python
import functools
import math

import jax
import jax.numpy as jnp
from jax import lax
from jax.experimental import pallas as pl
from jax.experimental.pallas import tpu as pltpu
from jax.sharding import Mesh, PartitionSpec as P

GRID = 5
BOX = 64
HALF = 1536
WIDTH = 3072
PARTS = 64
ROWS = 75
PAD = 80
LANES = 128
CHUNK = 384
GROUP = 8
NPART = PARTS * GROUP
SHIFTS = GRID * GRID
BLOCK = GRID * PAD
EXCLUDED = -1e30
SCALE = 1.0 / math.sqrt(WIDTH)
AXES = ("y", "xh", "z", "xl", "co")

f32 = jnp.float32
bf16 = jnp.bfloat16


def sin_cos(turns):
    quarter = jnp.floor(turns * (1.0 / 16.0) + 0.5)
    rest = (turns - 16.0 * quarter) * (2.0 * math.pi / BOX)
    sq = rest * rest
    sin = rest * (
        1.0 + sq * (-1.0 / 6 + sq * (1.0 / 120 + sq * (-1.0 / 5040 + sq * (1.0 / 362880))))
    )
    cos = 1.0 + sq * (
        -0.5 + sq * (1.0 / 24 + sq * (-1.0 / 720 + sq * (1.0 / 40320 + sq * (-1.0 / 3628800))))
    )
    quad = quarter - 4.0 * jnp.floor(quarter * 0.25)
    swap = (quad == 1.0) | (quad == 3.0)
    sin_q = jnp.where(swap, cos, sin)
    cos_q = jnp.where(swap, sin, cos)
    sin_q = jnp.where(quad >= 2.0, -sin_q, sin_q)
    cos_q = jnp.where((quad == 1.0) | (quad == 2.0), -cos_q, cos_q)
    return sin_q, cos_q


def prep_kernel(img_ref, off_ref, list_ref, w_ref, out_ref, half_ref, tab_ref):
    eye = jnp.where(
        lax.broadcasted_iota(jnp.int32, (PARTS, PARTS), 0)
        == lax.broadcasted_iota(jnp.int32, (PARTS, PARTS), 1),
        1.0,
        0.0,
    ).astype(bf16)

    def upright(ref):
        flat = ref[...].astype(f32).astype(bf16)
        return lax.dot_general(eye, flat, (((1,), (1,)), ((), ())), preferred_element_type=f32)

    off = upright(off_ref)
    ox, oy = off[:, 0:1], off[:, 1:2]
    first = lax.axis_index("co") == 0

    def put(lanes, value):
        value = value.astype(bf16)
        out_ref[:, lanes] = value
        half_ref[:, lanes] = jnp.where(first, value[: PARTS // 2], value[PARTS // 2 :])

    for t in range(HALF // LANES):
        lanes = slice(t * LANES, (t + 1) * LANES)
        ims = slice(HALF + t * LANES, HALF + (t + 1) * LANES)
        k = lax.broadcasted_iota(jnp.int32, (1, LANES), 1) + t * LANES
        kx = ((k & (BOX - 1)) - BOX // 2).astype(f32)
        ky = (k >> 6).astype(f32)
        sin, cos = sin_cos(ox * kx + oy * ky)
        a = img_ref[:, lanes].astype(f32)
        b = img_ref[:, ims].astype(f32)
        w = w_ref[lanes].reshape(1, LANES)
        put(lanes, w * (a * cos + b * sin))
        put(ims, w * (b * cos - a * sin))
        step = lax.broadcasted_iota(jnp.int32, (8, 1), 0)
        move = (((step >> 1) & 1) + 1).astype(f32)
        freq = jnp.where(step < 4, kx, ky)
        tab_sin, tab_cos = sin_cos(move * freq)
        tab_ref[0:8, lanes] = jnp.where((step & 1) == 0, tab_cos, tab_sin)
        tab_ref[8:16, lanes] = jnp.broadcast_to(w, (8, LANES))
    lists = upright(list_ref)
    lane = lax.broadcasted_iota(jnp.int32, (PARTS, LANES), 1).astype(f32)
    listed = lists[:, 0:1] == lane
    for n in range(1, lists.shape[1]):
        listed = listed | (lists[:, n : n + 1] == lane)
    put(slice(WIDTH, WIDTH + LANES), jnp.where(listed, 1.0, 0.0))


VMEM = pl.BlockSpec(memory_space=pltpu.VMEM)


def prep(images, offsets, class_lists, weight):
    return pl.pallas_call(
        prep_kernel,
        in_specs=[VMEM] * 4,
        out_specs=[VMEM] * 3,
        out_shape=[
            jax.ShapeDtypeStruct((PARTS, WIDTH + LANES), bf16),
            jax.ShapeDtypeStruct((PARTS // 2, WIDTH + LANES), bf16),
            jax.ShapeDtypeStruct((16, HALF), f32),
        ],
        compiler_params=pltpu.CompilerParams(vmem_limit_bytes=8 << 20),
        cost_estimate=pl.CostEstimate(flops=4 << 20, bytes_accessed=1 << 20, transcendentals=0),
    )(images, offsets, class_lists, weight)


def y_shift(tab_ref, gy, lanes):
    row = 2 + 2 * abs(gy)
    c = tab_ref[row : row + 1, lanes]
    s = tab_ref[row + 1 : row + 2, lanes]
    return c, (s if gy > 0 else -s)


def shift_kernel(*args):
    pieces, (tab_ref, out_ref, energy_ref, r_ref, total) = args[:4], args[4:]
    y, xh = lax.axis_index("y"), lax.axis_index("xh")
    for far, ref in enumerate(pieces):
        for n in range(2):
            place = ((y + 4 - far) & 3) * 2 + (xh if n == 0 else 1 - xh)
            at = pl.multiple_of(place * CHUNK, CHUNK)
            r_ref[pl.ds(at, CHUNK), :] = ref[n * CHUNK : (n + 1) * CHUNK, :]
    total[...] = jnp.zeros_like(total)
    for at in range(0, HALF, LANES):
        lanes, ims = slice(at, at + LANES), slice(HALF + at, HALF + at + LANES)
        all_re = r_ref[lanes, :].astype(f32).T[:PAD]
        all_im = r_ref[ims, :].astype(f32).T[:PAD]
        total[...] += (all_re * all_re + all_im * all_im) * tab_ref[8:9, lanes]
        for p in range(0, PAD, 16):
            for gy in range(-2, 3):
                yr, yi = all_re[p : p + 16], all_im[p : p + 16]
                if gy:
                    c, s = y_shift(tab_ref, gy, lanes)
                    yr, yi = yr * c - yi * s, yi * c + yr * s
                mid = ((gy + 2) * GRID + 2) * PAD + p
                out_ref[mid : mid + 16, lanes] = yr.astype(bf16)
                out_ref[mid : mid + 16, ims] = yi.astype(bf16)
                for gx in (1, 2):
                    c = tab_ref[2 * gx - 2 : 2 * gx - 1, lanes]
                    s = tab_ref[2 * gx - 1 : 2 * gx, lanes]
                    cr, ci, sr, si = yr * c, yi * c, yr * s, yi * s
                    hi = slice(mid + gx * PAD, mid + gx * PAD + 16)
                    lo = slice(mid - gx * PAD, mid - gx * PAD + 16)
                    out_ref[hi, lanes] = (cr - si).astype(bf16)
                    out_ref[hi, ims] = (ci + sr).astype(bf16)
                    out_ref[lo, lanes] = (cr + si).astype(bf16)
                    out_ref[lo, ims] = (ci - sr).astype(bf16)
    energy_ref[...] = jnp.broadcast_to(
        0.5 * jnp.sum(total[...], axis=1, keepdims=True), energy_ref.shape
    )


def shift_refs(refs, table):
    return pl.pallas_call(
        shift_kernel,
        in_specs=[VMEM] * 5,
        out_specs=[VMEM] * 2,
        out_shape=[
            jax.ShapeDtypeStruct((SHIFTS * PAD, WIDTH), bf16),
            jax.ShapeDtypeStruct((PAD, LANES), f32),
        ],
        scratch_shapes=[pltpu.VMEM((WIDTH, LANES), bf16), pltpu.VMEM((PAD, LANES), f32)],
        compiler_params=pltpu.CompilerParams(vmem_limit_bytes=16 << 20),
        cost_estimate=pl.CostEstimate(flops=1, bytes_accessed=1, transcendentals=0),
    )(*refs, table)


def assemble(pieces, probes):
    z, co = lax.axis_index("z"), lax.axis_index("co")
    half = PARTS // 2
    for ref, far, mine, skip, rows in pieces:
        at = ((z + far + GROUP) & (GROUP - 1)) * PARTS + skip
        if mine is not None:
            at = at + half * (co if mine else 1 - co)
        probes[pl.ds(pl.multiple_of(at, 16), rows), :] = ref[...]


def name_pieces(refs):
    half = PARTS // 2
    out = [(refs[0], 0, None, 0, PARTS)]
    for mine, part in ((True, refs[1:9]), (False, refs[9:17])):
        for n, far in enumerate((-1, -2, -3, 1, 2, 3)):
            out.append((part[n], far, mine, 0, half))
        out.append((part[6], 4, mine, 0, half // 2))
        out.append((part[7], 4, mine, half // 2, half // 2))
    return out


PIECES = 17


def estep_kernel(*args):
    pieces, (shifted, energy_ref, probes, expo_ref, stat_ref) = args[:PIECES], args[PIECES:]
    assemble(name_pieces(pieces), probes)
    cls = lax.axis_index("xl") * 2 + lax.axis_index("co")
    base = cls * (ROWS * GROUP) + lax.axis_index("z") * ROWS
    row = lax.broadcasted_iota(jnp.int32, (PAD, LANES), 0)
    number = ((base + row) * 2731) >> 16
    lane = lax.broadcasted_iota(jnp.int32, (PAD, LANES), 1)
    pick = jnp.where((number == lane) & (row < ROWS), 1.0, 0.0).astype(bf16)
    half_energy = energy_ref[:, 0:1]
    keep = (
        lax.dot_general(
            pick, probes[:, WIDTH:], (((1,), (1,)), ((), ())), preferred_element_type=f32
        )
        > 0.5
    )
    for b in range(GRID):
        cross = lax.dot_general(
            shifted[b * BLOCK : (b + 1) * BLOCK, :],
            probes[:, :WIDTH],
            (((1,), (1,)), ((), ())),
            preferred_element_type=f32,
        )
        best = jnp.full((8, NPART), EXCLUDED, f32)
        for gx in range(GRID):
            at = (b * GRID + gx) * PAD
            score = (cross[gx * PAD : (gx + 1) * PAD] - half_energy) * SCALE
            score = jnp.where(keep, score, EXCLUDED)
            expo_ref[at : at + PAD, :] = score
            best = jnp.maximum(best, jnp.max(score.reshape(PAD // 8, 8, NPART), axis=0))
        peak = jnp.max(best, axis=0, keepdims=True)
        mass = jnp.zeros((8, NPART), f32)
        for gx in range(GRID):
            at = (b * GRID + gx) * PAD
            e = jnp.where(keep, jnp.exp(expo_ref[at : at + PAD, :] - peak), 0.0)
            expo_ref[at : at + PAD, :] = e
            mass = mass + jnp.sum(e.reshape(PAD // 8, 8, NPART), axis=0)
        stat_ref[b : b + 1, :] = peak
        stat_ref[8 + b : 9 + b, :] = jnp.sum(mass, axis=0, keepdims=True)
    peaks = [stat_ref[b : b + 1, :] for b in range(GRID)]
    peak = functools.reduce(jnp.maximum, peaks)
    stat_ref[5:6, :] = peak
    stat_ref[6:7, :] = sum(
        stat_ref[8 + b : 9 + b, :] * jnp.exp(peaks[b] - peak) for b in range(GRID)
    )


def estep(pieces, shifted, energy):
    return pl.pallas_call(
        estep_kernel,
        in_specs=[VMEM] * (PIECES + 2),
        out_specs=[VMEM] * 3,
        out_shape=[
            jax.ShapeDtypeStruct((NPART, WIDTH + LANES), bf16),
            jax.ShapeDtypeStruct((SHIFTS * PAD, NPART), f32),
            jax.ShapeDtypeStruct((16, NPART), f32),
        ],
        compiler_params=pltpu.CompilerParams(vmem_limit_bytes=30 << 20),
        cost_estimate=pl.CostEstimate(
            flops=2 * SHIFTS * PAD * NPART * WIDTH,
            bytes_accessed=24 << 20,
            transcendentals=SHIFTS * PAD * NPART,
        ),
    )(*pieces, shifted, energy)


STRIP = 256


def mstep_kernel(stat_ref, all_ref, p_ref, expo_ref, tab_ref, out_ref, post, sums):
    count = all_ref.shape[0]
    peak = all_ref[0, 0:1, :]
    for d in range(1, count):
        peak = jnp.maximum(peak, all_ref[d, 0:1, :])
    mass = jnp.zeros((1, NPART), f32)
    for d in range(count):
        mass = mass + all_ref[d, 1:2, :] * jnp.exp(all_ref[d, 0:1, :] - peak)
    inverse = 1.0 / mass
    for b in range(GRID):
        rows = slice(b * BLOCK, (b + 1) * BLOCK)
        factor = jnp.exp(stat_ref[b : b + 1, :] - peak) * inverse
        post[rows, :] = (expo_ref[rows, :] * factor).astype(bf16)
    turn = 0
    for strip in range(HALF // STRIP):
        re_cols = slice(strip * STRIP, (strip + 1) * STRIP)
        im_cols = slice(HALF + strip * STRIP, HALF + (strip + 1) * STRIP)
        for b in range(GRID):
            rows = slice(b * BLOCK, (b + 1) * BLOCK)
            k = turn % 2
            turn += 1
            sums[k, :, :STRIP] = jnp.dot(
                post[rows, :], p_ref[:, re_cols], preferred_element_type=f32
            )
            sums[k, :, STRIP:] = jnp.dot(
                post[rows, :], p_ref[:, im_cols], preferred_element_type=f32
            )
            for t in range(STRIP // LANES):
                at = strip * STRIP + t * LANES
                lanes = slice(at, at + LANES)
                res = slice(t * LANES, (t + 1) * LANES)
                ims = slice(STRIP + t * LANES, STRIP + (t + 1) * LANES)
                re = sums[k, 2 * PAD : 3 * PAD, res]
                im = sums[k, 2 * PAD : 3 * PAD, ims]
                for gx in (1, 2):
                    c = tab_ref[2 * gx - 2 : 2 * gx - 1, lanes]
                    s = tab_ref[2 * gx - 1 : 2 * gx, lanes]
                    hi = slice((2 + gx) * PAD, (3 + gx) * PAD)
                    lo = slice((2 - gx) * PAD, (3 - gx) * PAD)
                    pr, pi = sums[k, hi, res], sums[k, hi, ims]
                    mr, mi = sums[k, lo, res], sums[k, lo, ims]
                    re = re + c * (pr + mr) + s * (pi - mi)
                    im = im + c * (pi + mi) - s * (pr - mr)
                if b != 2:
                    cy, sy = y_shift(tab_ref, b - 2, lanes)
                    re, im = re * cy + im * sy, im * cy - re * sy
                g, chunk = at // CHUNK, slice(at % CHUNK, at % CHUNK + LANES)
                if b == 0:
                    out_ref[g, :, chunk] = re
                    out_ref[g + 4, :, chunk] = im
                else:
                    out_ref[g, :, chunk] += re
                    out_ref[g + 4, :, chunk] += im


def mstep(stat, stats, probes, expo, table):
    return pl.pallas_call(
        mstep_kernel,
        in_specs=[VMEM] * 5,
        out_specs=VMEM,
        out_shape=jax.ShapeDtypeStruct((GROUP, PAD, CHUNK), f32),
        scratch_shapes=[
            pltpu.VMEM((SHIFTS * PAD, NPART), bf16),
            pltpu.VMEM((2, BLOCK, 2 * STRIP), f32),
        ],
        compiler_params=pltpu.CompilerParams(vmem_limit_bytes=20 << 20),
        cost_estimate=pl.CostEstimate(
            flops=2 * SHIFTS * PAD * NPART * WIDTH, bytes_accessed=9 << 20, transcendentals=0
        ),
    )(stat, stats, probes, expo, table)


def along_z(x, far):
    return lax.ppermute(x, "z", [(i, (i + far) % GROUP) for i in range(GROUP)])


def to_other_core(x):
    return lax.ppermute(x, "co", [(0, 1), (1, 0)])


def per_device(images, offsets, class_lists, noise_weight, references):
    own, half, table = prep(images, offsets.T, class_lists.T, noise_weight)

    part = references.reshape(GROUP, ROWS, 48)
    part = jnp.pad(jnp.transpose(part, (0, 2, 1)), ((0, 0), (0, 0), (0, LANES - ROWS)))
    part = lax.all_to_all(part, "z", 0, 0).reshape(CHUNK, LANES)
    part, table = lax.optimization_barrier((part, table))
    part = jnp.concatenate([part, lax.ppermute(part, "xh", [(0, 1), (1, 0)])])
    refs = [part]
    for far in (1, 2, 3):
        refs.append(lax.ppermute(part, "y", [(i, (i + far) % 4) for i in range(4)]))
    shifted, energy = shift_refs(refs, table)

    up, down = [half], [half]
    for _ in range(3):
        up.append(along_z(up[-1], 1))
        down.append(along_z(down[-1], -1))
    cut = PARTS // 4
    mine = up[1:] + down[1:] + [along_z(up[-1][:cut], 1), along_z(down[-1][cut:], -1)]
    mine[6], mine[7], shifted = lax.optimization_barrier((mine[6], mine[7], shifted))
    pieces = [own] + mine + [to_other_core(x) for x in mine]

    probes, expo, stat = estep(pieces, shifted, energy)
    stats = lax.all_to_all(
        jnp.broadcast_to(stat[5:7], (32, 2, NPART)), ("z", "xl", "co"), 0, 0
    )
    sums = mstep(stat, stats, probes, expo, table)

    sums = jnp.sum(lax.all_to_all(sums, ("y", "xh"), 0, 0), axis=0)
    sums = jnp.pad(sums.T, ((0, 0), (0, LANES - PAD))).reshape(GROUP, 48, LANES)
    sums = lax.all_to_all(sums, "z", 0, 0)[:, :, :ROWS]
    return jnp.transpose(sums, (1, 0, 2)).reshape(48, GROUP * ROWS)


def solution(mesh):
    fine = Mesh(mesh.devices.reshape(4, 2, 8, 2, 2), AXES)
    dom, cls = ("y", "xh", "z"), ("xl", "co")
    in_specs = (P(dom, None), P(dom, None), P(dom, None), P(), P(cls, None, dom))
    return jax.shard_map(
        per_device, mesh=fine, in_specs=in_specs, out_specs=P(dom, cls), check_vma=False
    )
```

```python
import functools
import math

import jax
import jax.numpy as jnp
from jax import lax
from jax.experimental import pallas as pl
from jax.experimental.pallas import tpu as pltpu
from jax.sharding import Mesh, PartitionSpec as P

GRID = 5
BOX = 64
HALF = 1536
WIDTH = 3072
PARTS = 64
ROWS = 75
PAD = 80
LANES = 128
CHUNK = 384
GROUP = 8
NPART = PARTS * GROUP
SHIFTS = GRID * GRID
BLOCK = GRID * PAD
EXCLUDED = -1e30
SCALE = 1.0 / math.sqrt(WIDTH)
AXES = ("y", "xh", "z", "xl", "co")

f32 = jnp.float32
bf16 = jnp.bfloat16


def sin_cos(turns):
    quarter = jnp.floor(turns * (1.0 / 16.0) + 0.5)
    rest = (turns - 16.0 * quarter) * (2.0 * math.pi / BOX)
    sq = rest * rest
    sin = rest * (
        1.0 + sq * (-1.0 / 6 + sq * (1.0 / 120 + sq * (-1.0 / 5040 + sq * (1.0 / 362880))))
    )
    cos = 1.0 + sq * (
        -0.5 + sq * (1.0 / 24 + sq * (-1.0 / 720 + sq * (1.0 / 40320 + sq * (-1.0 / 3628800))))
    )
    quad = quarter - 4.0 * jnp.floor(quarter * 0.25)
    swap = (quad == 1.0) | (quad == 3.0)
    sin_q = jnp.where(swap, cos, sin)
    cos_q = jnp.where(swap, sin, cos)
    sin_q = jnp.where(quad >= 2.0, -sin_q, sin_q)
    cos_q = jnp.where((quad == 1.0) | (quad == 2.0), -cos_q, cos_q)
    return sin_q, cos_q


def prep_kernel(img_ref, off_ref, list_ref, w_ref, out_ref, half_ref, tab_ref):
    eye = jnp.where(
        lax.broadcasted_iota(jnp.int32, (PARTS, PARTS), 0)
        == lax.broadcasted_iota(jnp.int32, (PARTS, PARTS), 1),
        1.0,
        0.0,
    ).astype(bf16)

    def upright(ref):
        flat = ref[...].astype(f32).astype(bf16)
        return lax.dot_general(eye, flat, (((1,), (1,)), ((), ())), preferred_element_type=f32)

    off = upright(off_ref)
    ox, oy = off[:, 0:1], off[:, 1:2]
    first = lax.axis_index("co") == 0

    def put(lanes, value):
        value = value.astype(bf16)
        out_ref[:, lanes] = value
        half_ref[:, lanes] = jnp.where(first, value[: PARTS // 2], value[PARTS // 2 :])

    for t in range(HALF // LANES):
        lanes = slice(t * LANES, (t + 1) * LANES)
        ims = slice(HALF + t * LANES, HALF + (t + 1) * LANES)
        k = lax.broadcasted_iota(jnp.int32, (1, LANES), 1) + t * LANES
        kx = ((k & (BOX - 1)) - BOX // 2).astype(f32)
        ky = (k >> 6).astype(f32)
        sin, cos = sin_cos(ox * kx + oy * ky)
        a = img_ref[:, lanes].astype(f32)
        b = img_ref[:, ims].astype(f32)
        w = w_ref[lanes].reshape(1, LANES)
        put(lanes, w * (a * cos + b * sin))
        put(ims, w * (b * cos - a * sin))
        step = lax.broadcasted_iota(jnp.int32, (8, 1), 0)
        move = (((step >> 1) & 1) + 1).astype(f32)
        freq = jnp.where(step < 4, kx, ky)
        tab_sin, tab_cos = sin_cos(move * freq)
        tab_ref[0:8, lanes] = jnp.where((step & 1) == 0, tab_cos, tab_sin)
        tab_ref[8:16, lanes] = jnp.broadcast_to(w, (8, LANES))
    lists = upright(list_ref)
    lane = lax.broadcasted_iota(jnp.int32, (PARTS, LANES), 1).astype(f32)
    listed = lists[:, 0:1] == lane
    for n in range(1, lists.shape[1]):
        listed = listed | (lists[:, n : n + 1] == lane)
    put(slice(WIDTH, WIDTH + LANES), jnp.where(listed, 1.0, 0.0))


VMEM = pl.BlockSpec(memory_space=pltpu.VMEM)


def prep(images, offsets, class_lists, weight):
    return pl.pallas_call(
        prep_kernel,
        in_specs=[VMEM] * 4,
        out_specs=[VMEM] * 3,
        out_shape=[
            jax.ShapeDtypeStruct((PARTS, WIDTH + LANES), bf16),
            jax.ShapeDtypeStruct((PARTS // 2, WIDTH + LANES), bf16),
            jax.ShapeDtypeStruct((16, HALF), f32),
        ],
        compiler_params=pltpu.CompilerParams(vmem_limit_bytes=8 << 20),
        cost_estimate=pl.CostEstimate(flops=4 << 20, bytes_accessed=1 << 20, transcendentals=0),
    )(images, offsets, class_lists, weight)


COLS = 48


def split_kernel(ref_ref, out_ref, tall):
    tall[...] = jnp.zeros_like(tall)
    tall[: GROUP * ROWS, :COLS] = ref_ref[...].astype(f32).reshape(GROUP * ROWS, COLS)
    flat = tall[...].T[:COLS]
    lane = lax.broadcasted_iota(jnp.int32, (COLS, LANES), 1)
    for m in range(GROUP):
        part = flat[:, m * ROWS : m * ROWS + LANES]
        out_ref[m] = jnp.where(lane < ROWS, part, 0.0).astype(bf16)


def split_refs(references):
    return pl.pallas_call(
        split_kernel,
        in_specs=[VMEM],
        out_specs=VMEM,
        out_shape=jax.ShapeDtypeStruct((GROUP, COLS, LANES), bf16),
        scratch_shapes=[pltpu.VMEM((6 * LANES, LANES), f32)],
        compiler_params=pltpu.CompilerParams(vmem_limit_bytes=8 << 20),
        cost_estimate=pl.CostEstimate(flops=1 << 20, bytes_accessed=1 << 20, transcendentals=0),
    )(references)


def y_shift(tab_ref, gy, lanes):
    row = 2 + 2 * abs(gy)
    c = tab_ref[row : row + 1, lanes]
    s = tab_ref[row + 1 : row + 2, lanes]
    return c, (s if gy > 0 else -s)


def columns_last(pieces, tab_ref, base, total):
    y, xh = lax.axis_index("y"), lax.axis_index("xh")
    total[...] = jnp.zeros_like(total)
    for far, ref in enumerate(pieces):
        for n in range(2):
            place = ((y + 4 - far) & 3) * 2 + (xh if n == 0 else 1 - xh)
            for t in range(CHUNK // LANES):
                at = place * CHUNK + t * LANES
                lanes = pl.ds(pl.multiple_of(at, LANES), LANES)
                wide = pl.ds(pl.multiple_of(at - HALF * (place >= 4), LANES), LANES)
                row = n * CHUNK + t * LANES
                value = ref[row : row + LANES, :].astype(f32).T[:PAD]
                base[:, lanes] = value
                total[...] += value * value * tab_ref[8:9, wide]


def shift_block(gy, tab_ref, base, out_ref):
    for at in range(0, HALF, LANES):
        lanes, ims = slice(at, at + LANES), slice(HALF + at, HALF + at + LANES)
        for p in range(0, PAD, 16):
            yr, yi = base[p : p + 16, lanes], base[p : p + 16, ims]
            if gy:
                c, s = y_shift(tab_ref, gy, lanes)
                yr, yi = yr * c - yi * s, yi * c + yr * s
            mid = 2 * PAD + p
            out_ref[mid : mid + 16, lanes] = yr.astype(bf16)
            out_ref[mid : mid + 16, ims] = yi.astype(bf16)
            for gx in (1, 2):
                c = tab_ref[2 * gx - 2 : 2 * gx - 1, lanes]
                s = tab_ref[2 * gx - 1 : 2 * gx, lanes]
                cr, ci, sr, si = yr * c, yi * c, yr * s, yi * s
                hi = slice(mid + gx * PAD, mid + gx * PAD + 16)
                lo = slice(mid - gx * PAD, mid - gx * PAD + 16)
                out_ref[hi, lanes] = (cr - si).astype(bf16)
                out_ref[hi, ims] = (ci + sr).astype(bf16)
                out_ref[lo, lanes] = (cr + si).astype(bf16)
                out_ref[lo, ims] = (ci - sr).astype(bf16)


def assemble(pieces, probes):
    z, co = lax.axis_index("z"), lax.axis_index("co")
    half = PARTS // 2
    for ref, far, mine, skip, rows in pieces:
        at = ((z + far + GROUP) & (GROUP - 1)) * PARTS + skip
        if mine is not None:
            at = at + half * (co if mine else 1 - co)
        probes[pl.ds(pl.multiple_of(at, 16), rows), :] = ref[...]


def name_pieces(refs):
    half = PARTS // 2
    out = [(refs[0], 0, None, 0, PARTS)]
    for mine, part in ((True, refs[1:9]), (False, refs[9:17])):
        for n, far in enumerate((-1, -2, -3, 1, 2, 3)):
            out.append((part[n], far, mine, 0, half))
        out.append((part[6], 4, mine, 0, half // 2))
        out.append((part[7], 4, mine, half // 2, half // 2))
    return out


PIECES = 17


def estep_kernel(*args):
    pieces, refs = args[:PIECES], args[PIECES : PIECES + 4]
    tab_ref, probes, expo_ref, stat_ref, base, total, *shifted = args[PIECES + 4 :]
    columns_last(refs, tab_ref, base, total)
    shift_block(-2, tab_ref, base, shifted[0])
    assemble(name_pieces(pieces), probes)
    cls = lax.axis_index("xl") * 2 + lax.axis_index("co")
    first_row = cls * (ROWS * GROUP) + lax.axis_index("z") * ROWS
    row = lax.broadcasted_iota(jnp.int32, (PAD, LANES), 0)
    number = ((first_row + row) * 2731) >> 16
    lane = lax.broadcasted_iota(jnp.int32, (PAD, LANES), 1)
    pick = jnp.where((number == lane) & (row < ROWS), 1.0, 0.0).astype(bf16)
    half_energy = 0.5 * jnp.sum(total[...], axis=1, keepdims=True)
    keep = (
        lax.dot_general(
            pick, probes[:, WIDTH:], (((1,), (1,)), ((), ())), preferred_element_type=f32
        )
        > 0.5
    )
    for b in range(GRID):
        cross = lax.dot_general(
            shifted[b % 2][...],
            probes[:, :WIDTH],
            (((1,), (1,)), ((), ())),
            preferred_element_type=f32,
        )
        if b < GRID - 1:
            shift_block(b - 1, tab_ref, base, shifted[(b + 1) % 2])
        best = jnp.full((8, NPART), EXCLUDED, f32)
        for gx in range(GRID):
            at = (b * GRID + gx) * PAD
            score = (cross[gx * PAD : (gx + 1) * PAD] - half_energy) * SCALE
            score = jnp.where(keep, score, EXCLUDED)
            expo_ref[at : at + PAD, :] = score
            best = jnp.maximum(best, jnp.max(score.reshape(PAD // 8, 8, NPART), axis=0))
        peak = jnp.max(best, axis=0, keepdims=True)
        mass = jnp.zeros((8, NPART), f32)
        for gx in range(GRID):
            at = (b * GRID + gx) * PAD
            e = jnp.where(keep, jnp.exp(expo_ref[at : at + PAD, :] - peak), 0.0)
            expo_ref[at : at + PAD, :] = e
            mass = mass + jnp.sum(e.reshape(PAD // 8, 8, NPART), axis=0)
        stat_ref[b : b + 1, :] = peak
        stat_ref[8 + b : 9 + b, :] = jnp.sum(mass, axis=0, keepdims=True)
    peaks = [stat_ref[b : b + 1, :] for b in range(GRID)]
    peak = functools.reduce(jnp.maximum, peaks)
    stat_ref[5:6, :] = peak
    stat_ref[6:7, :] = sum(
        stat_ref[8 + b : 9 + b, :] * jnp.exp(peaks[b] - peak) for b in range(GRID)
    )


def estep(pieces, refs, table):
    return pl.pallas_call(
        estep_kernel,
        in_specs=[VMEM] * (PIECES + 5),
        out_specs=[VMEM] * 3,
        out_shape=[
            jax.ShapeDtypeStruct((NPART, WIDTH + LANES), bf16),
            jax.ShapeDtypeStruct((SHIFTS * PAD, NPART), f32),
            jax.ShapeDtypeStruct((16, NPART), f32),
        ],
        scratch_shapes=[
            pltpu.VMEM((PAD, WIDTH), f32),
            pltpu.VMEM((PAD, LANES), f32),
            pltpu.VMEM((BLOCK, WIDTH), bf16),
            pltpu.VMEM((BLOCK, WIDTH), bf16),
        ],
        compiler_params=pltpu.CompilerParams(vmem_limit_bytes=30 << 20),
        cost_estimate=pl.CostEstimate(
            flops=2 * SHIFTS * PAD * NPART * WIDTH,
            bytes_accessed=24 << 20,
            transcendentals=SHIFTS * PAD * NPART,
        ),
    )(*pieces, *refs, table)


STRIP = 256


def mstep_kernel(stat_ref, all_ref, p_ref, expo_ref, tab_ref, out_ref, post, sums):
    count = all_ref.shape[0]
    peak = all_ref[0, 0:1, :]
    for d in range(1, count):
        peak = jnp.maximum(peak, all_ref[d, 0:1, :])
    mass = jnp.zeros((1, NPART), f32)
    for d in range(count):
        mass = mass + all_ref[d, 1:2, :] * jnp.exp(all_ref[d, 0:1, :] - peak)
    inverse = 1.0 / mass
    for b in range(GRID):
        rows = slice(b * BLOCK, (b + 1) * BLOCK)
        factor = jnp.exp(stat_ref[b : b + 1, :] - peak) * inverse
        post[rows, :] = (expo_ref[rows, :] * factor).astype(bf16)
    turn = 0
    for strip in range(HALF // STRIP):
        re_cols = slice(strip * STRIP, (strip + 1) * STRIP)
        im_cols = slice(HALF + strip * STRIP, HALF + (strip + 1) * STRIP)
        for b in range(GRID):
            rows = slice(b * BLOCK, (b + 1) * BLOCK)
            k = turn % 2
            turn += 1
            sums[k, :, :STRIP] = jnp.dot(
                post[rows, :], p_ref[:, re_cols], preferred_element_type=f32
            )
            sums[k, :, STRIP:] = jnp.dot(
                post[rows, :], p_ref[:, im_cols], preferred_element_type=f32
            )
            for t in range(STRIP // LANES):
                at = strip * STRIP + t * LANES
                lanes = slice(at, at + LANES)
                res = slice(t * LANES, (t + 1) * LANES)
                ims = slice(STRIP + t * LANES, STRIP + (t + 1) * LANES)
                re = sums[k, 2 * PAD : 3 * PAD, res]
                im = sums[k, 2 * PAD : 3 * PAD, ims]
                for gx in (1, 2):
                    c = tab_ref[2 * gx - 2 : 2 * gx - 1, lanes]
                    s = tab_ref[2 * gx - 1 : 2 * gx, lanes]
                    hi = slice((2 + gx) * PAD, (3 + gx) * PAD)
                    lo = slice((2 - gx) * PAD, (3 - gx) * PAD)
                    pr, pi = sums[k, hi, res], sums[k, hi, ims]
                    mr, mi = sums[k, lo, res], sums[k, lo, ims]
                    re = re + c * (pr + mr) + s * (pi - mi)
                    im = im + c * (pi + mi) - s * (pr - mr)
                if b != 2:
                    cy, sy = y_shift(tab_ref, b - 2, lanes)
                    re, im = re * cy + im * sy, im * cy - re * sy
                g, chunk = at // CHUNK, slice(at % CHUNK, at % CHUNK + LANES)
                if b == 0:
                    out_ref[g, :, chunk] = re
                    out_ref[g + 4, :, chunk] = im
                else:
                    out_ref[g, :, chunk] += re
                    out_ref[g + 4, :, chunk] += im


def mstep(stat, stats, probes, expo, table):
    return pl.pallas_call(
        mstep_kernel,
        in_specs=[VMEM] * 5,
        out_specs=VMEM,
        out_shape=jax.ShapeDtypeStruct((GROUP, PAD, CHUNK), f32),
        scratch_shapes=[
            pltpu.VMEM((SHIFTS * PAD, NPART), bf16),
            pltpu.VMEM((2, BLOCK, 2 * STRIP), f32),
        ],
        compiler_params=pltpu.CompilerParams(vmem_limit_bytes=20 << 20),
        cost_estimate=pl.CostEstimate(
            flops=2 * SHIFTS * PAD * NPART * WIDTH, bytes_accessed=9 << 20, transcendentals=0
        ),
    )(stat, stats, probes, expo, table)


def along_z(x, far):
    return lax.ppermute(x, "z", [(i, (i + far) % GROUP) for i in range(GROUP)])


def to_other_core(x):
    return lax.ppermute(x, "co", [(0, 1), (1, 0)])


def per_device(images, offsets, class_lists, noise_weight, references):
    own, half, table = prep(images, offsets.T, class_lists.T, noise_weight)

    part = split_refs(references)
    part = lax.all_to_all(part, "z", 0, 0).reshape(CHUNK, LANES)
    part, table = lax.optimization_barrier((part, table))
    part = jnp.concatenate([part, lax.ppermute(part, "xh", [(0, 1), (1, 0)])])
    refs = [part]
    for far in (1, 2, 3):
        refs.append(lax.ppermute(part, "y", [(i, (i + far) % 4) for i in range(4)]))

    up, down = [half], [half]
    for _ in range(3):
        up.append(along_z(up[-1], 1))
        down.append(along_z(down[-1], -1))
    cut = PARTS // 4
    mine = up[1:] + down[1:] + [along_z(up[-1][:cut], 1), along_z(down[-1][cut:], -1)]
    mine[6], mine[7], *refs = lax.optimization_barrier((mine[6], mine[7], *refs))
    pieces = [own] + mine + [to_other_core(x) for x in mine]

    probes, expo, stat = estep(pieces, refs, table)
    stats = lax.all_to_all(
        jnp.broadcast_to(stat[5:7], (32, 2, NPART)), ("z", "xl", "co"), 0, 0
    )
    sums = mstep(stat, stats, probes, expo, table)

    sums = jnp.sum(lax.all_to_all(sums, ("y", "xh"), 0, 0), axis=0)
    sums = jnp.pad(sums.T, ((0, 0), (0, LANES - PAD))).reshape(GROUP, 48, LANES)
    sums = lax.all_to_all(sums, "z", 0, 0)[:, :, :ROWS]
    return jnp.transpose(sums, (1, 0, 2)).reshape(48, GROUP * ROWS)


def solution(mesh):
    fine = Mesh(mesh.devices.reshape(4, 2, 8, 2, 2), AXES)
    dom, cls = ("y", "xh", "z"), ("xl", "co")
    in_specs = (P(dom, None), P(dom, None), P(dom, None), P(), P(cls, None, dom))
    return jax.shard_map(
        per_device, mesh=fine, in_specs=in_specs, out_specs=P(dom, cls), check_vma=False
    )
```

```python
import functools
import math

import jax
import jax.numpy as jnp
from jax import lax
from jax.experimental import pallas as pl
from jax.experimental.pallas import tpu as pltpu
from jax.sharding import Mesh, PartitionSpec as P

GRID = 5
BOX = 64
HALF = 1536
WIDTH = 3072
PARTS = 64
ROWS = 75
PAD = 80
LANES = 128
CHUNK = 384
GROUP = 8
NPART = PARTS * GROUP
SHIFTS = GRID * GRID
BLOCK = GRID * PAD
EXCLUDED = -1e30
SCALE = 1.0 / math.sqrt(WIDTH)
AXES = ("y", "xh", "z", "xl", "co")

f32 = jnp.float32
bf16 = jnp.bfloat16


def sin_cos(turns):
    quarter = jnp.floor(turns * (1.0 / 16.0) + 0.5)
    rest = (turns - 16.0 * quarter) * (2.0 * math.pi / BOX)
    sq = rest * rest
    sin = rest * (
        1.0 + sq * (-1.0 / 6 + sq * (1.0 / 120 + sq * (-1.0 / 5040 + sq * (1.0 / 362880))))
    )
    cos = 1.0 + sq * (
        -0.5 + sq * (1.0 / 24 + sq * (-1.0 / 720 + sq * (1.0 / 40320 + sq * (-1.0 / 3628800))))
    )
    quad = quarter - 4.0 * jnp.floor(quarter * 0.25)
    swap = (quad == 1.0) | (quad == 3.0)
    sin_q = jnp.where(swap, cos, sin)
    cos_q = jnp.where(swap, sin, cos)
    sin_q = jnp.where(quad >= 2.0, -sin_q, sin_q)
    cos_q = jnp.where((quad == 1.0) | (quad == 2.0), -cos_q, cos_q)
    return sin_q, cos_q


def prep_kernel(img_ref, off_ref, list_ref, w_ref, out_ref, half_ref, tab_ref):
    eye = jnp.where(
        lax.broadcasted_iota(jnp.int32, (PARTS, PARTS), 0)
        == lax.broadcasted_iota(jnp.int32, (PARTS, PARTS), 1),
        1.0,
        0.0,
    ).astype(bf16)

    def upright(ref):
        flat = ref[...].astype(f32).astype(bf16)
        return lax.dot_general(eye, flat, (((1,), (1,)), ((), ())), preferred_element_type=f32)

    off = upright(off_ref)
    ox, oy = off[:, 0:1], off[:, 1:2]
    first = lax.axis_index("co") == 0

    def put(lanes, value):
        value = value.astype(bf16)
        out_ref[:, lanes] = value
        half_ref[:, lanes] = jnp.where(first, value[: PARTS // 2], value[PARTS // 2 :])

    for t in range(HALF // LANES):
        lanes = slice(t * LANES, (t + 1) * LANES)
        ims = slice(HALF + t * LANES, HALF + (t + 1) * LANES)
        k = lax.broadcasted_iota(jnp.int32, (1, LANES), 1) + t * LANES
        kx = ((k & (BOX - 1)) - BOX // 2).astype(f32)
        ky = (k >> 6).astype(f32)
        sin, cos = sin_cos(ox * kx + oy * ky)
        a = img_ref[:, lanes].astype(f32)
        b = img_ref[:, ims].astype(f32)
        w = w_ref[lanes].reshape(1, LANES)
        put(lanes, w * (a * cos + b * sin))
        put(ims, w * (b * cos - a * sin))
        step = lax.broadcasted_iota(jnp.int32, (8, 1), 0)
        move = (((step >> 1) & 1) + 1).astype(f32)
        freq = jnp.where(step < 4, kx, ky)
        tab_sin, tab_cos = sin_cos(move * freq)
        tab_ref[0:8, lanes] = jnp.where((step & 1) == 0, tab_cos, tab_sin)
        tab_ref[8:16, lanes] = jnp.broadcast_to(w, (8, LANES))
    lists = upright(list_ref)
    lane = lax.broadcasted_iota(jnp.int32, (PARTS, LANES), 1).astype(f32)
    listed = lists[:, 0:1] == lane
    for n in range(1, lists.shape[1]):
        listed = listed | (lists[:, n : n + 1] == lane)
    put(slice(WIDTH, WIDTH + LANES), jnp.where(listed, 1.0, 0.0))


VMEM = pl.BlockSpec(memory_space=pltpu.VMEM)


def prep(images, offsets, class_lists, weight):
    return pl.pallas_call(
        prep_kernel,
        in_specs=[VMEM] * 4,
        out_specs=[VMEM] * 3,
        out_shape=[
            jax.ShapeDtypeStruct((PARTS, WIDTH + LANES), bf16),
            jax.ShapeDtypeStruct((PARTS // 2, WIDTH + LANES), bf16),
            jax.ShapeDtypeStruct((16, HALF), f32),
        ],
        compiler_params=pltpu.CompilerParams(vmem_limit_bytes=8 << 20),
        cost_estimate=pl.CostEstimate(flops=4 << 20, bytes_accessed=1 << 20, transcendentals=0),
    )(images, offsets, class_lists, weight)


COLS = 48


def split_kernel(ref_ref, out_ref, tall):
    tall[...] = jnp.zeros_like(tall)
    tall[: GROUP * ROWS, :COLS] = ref_ref[...].astype(f32).reshape(GROUP * ROWS, COLS)
    flat = tall[...].T[:COLS]
    lane = lax.broadcasted_iota(jnp.int32, (COLS, LANES), 1)
    for m in range(GROUP):
        part = flat[:, m * ROWS : m * ROWS + LANES]
        out_ref[m] = jnp.where(lane < ROWS, part, 0.0).astype(bf16)


def split_refs(references):
    return pl.pallas_call(
        split_kernel,
        in_specs=[VMEM],
        out_specs=VMEM,
        out_shape=jax.ShapeDtypeStruct((GROUP, COLS, LANES), bf16),
        scratch_shapes=[pltpu.VMEM((6 * LANES, LANES), f32)],
        compiler_params=pltpu.CompilerParams(vmem_limit_bytes=8 << 20),
        cost_estimate=pl.CostEstimate(flops=1 << 20, bytes_accessed=1 << 20, transcendentals=0),
    )(references)


def y_shift(tab_ref, gy, lanes):
    row = 2 + 2 * abs(gy)
    c = tab_ref[row : row + 1, lanes]
    s = tab_ref[row + 1 : row + 2, lanes]
    return c, (s if gy > 0 else -s)


def columns_last(pieces, tab_ref, base, total):
    y, xh = lax.axis_index("y"), lax.axis_index("xh")
    total[...] = jnp.zeros_like(total)
    for far, ref in enumerate(pieces):
        for n in range(2):
            place = ((y + 4 - far) & 3) * 2 + (xh if n == 0 else 1 - xh)
            for t in range(CHUNK // LANES):
                at = place * CHUNK + t * LANES
                lanes = pl.ds(pl.multiple_of(at, LANES), LANES)
                wide = pl.ds(pl.multiple_of(at - HALF * (place >= 4), LANES), LANES)
                row = n * CHUNK + t * LANES
                value = ref[row : row + LANES, :].astype(f32).T[:PAD]
                base[:, lanes] = value
                total[...] += value * value * tab_ref[8:9, wide]


def shift_block(gy, tab_ref, base, out_ref, first=0, end=HALF):
    for at in range(first, end, LANES):
        lanes, ims = slice(at, at + LANES), slice(HALF + at, HALF + at + LANES)
        for p in range(0, PAD, 16):
            yr, yi = base[p : p + 16, lanes], base[p : p + 16, ims]
            if gy:
                c, s = y_shift(tab_ref, gy, lanes)
                yr, yi = yr * c - yi * s, yi * c + yr * s
            mid = 2 * PAD + p
            out_ref[mid : mid + 16, lanes] = yr.astype(bf16)
            out_ref[mid : mid + 16, ims] = yi.astype(bf16)
            for gx in (1, 2):
                c = tab_ref[2 * gx - 2 : 2 * gx - 1, lanes]
                s = tab_ref[2 * gx - 1 : 2 * gx, lanes]
                cr, ci, sr, si = yr * c, yi * c, yr * s, yi * s
                hi = slice(mid + gx * PAD, mid + gx * PAD + 16)
                lo = slice(mid - gx * PAD, mid - gx * PAD + 16)
                out_ref[hi, lanes] = (cr - si).astype(bf16)
                out_ref[hi, ims] = (ci + sr).astype(bf16)
                out_ref[lo, lanes] = (cr + si).astype(bf16)
                out_ref[lo, ims] = (ci - sr).astype(bf16)


def assemble(pieces, probes):
    z, co = lax.axis_index("z"), lax.axis_index("co")
    half = PARTS // 2
    for ref, far, mine, skip, rows in pieces:
        at = ((z + far + GROUP) & (GROUP - 1)) * PARTS + skip
        if mine is not None:
            at = at + half * (co if mine else 1 - co)
        probes[pl.ds(pl.multiple_of(at, 16), rows), :] = ref[...]


def name_pieces(refs):
    half = PARTS // 2
    out = [(refs[0], 0, None, 0, PARTS)]
    for mine, part in ((True, refs[1:9]), (False, refs[9:17])):
        for n, far in enumerate((-1, -2, -3, 1, 2, 3)):
            out.append((part[n], far, mine, 0, half))
        out.append((part[6], 4, mine, 0, half // 2))
        out.append((part[7], 4, mine, half // 2, half // 2))
    return out


PIECES = 17


def estep_kernel(*args):
    pieces, refs = args[:PIECES], args[PIECES : PIECES + 4]
    tab_ref, probes, expo_ref, stat_ref, base, total, *shifted = args[PIECES + 4 :]
    columns_last(refs, tab_ref, base, total)
    shift_block(-2, tab_ref, base, shifted[0])
    assemble(name_pieces(pieces), probes)
    cls = lax.axis_index("xl") * 2 + lax.axis_index("co")
    first_row = cls * (ROWS * GROUP) + lax.axis_index("z") * ROWS
    row = lax.broadcasted_iota(jnp.int32, (PAD, LANES), 0)
    number = ((first_row + row) * 2731) >> 16
    lane = lax.broadcasted_iota(jnp.int32, (PAD, LANES), 1)
    pick = jnp.where((number == lane) & (row < ROWS), 1.0, 0.0).astype(bf16)
    half_energy = 0.5 * jnp.sum(total[...], axis=1, keepdims=True)
    keep = (
        lax.dot_general(
            pick, probes[:, WIDTH:], (((1,), (1,)), ((), ())), preferred_element_type=f32
        )
        > 0.5
    )
    for b in range(GRID):
        cross = []
        for h in range(2):
            cross.append(
                lax.dot_general(
                    shifted[b % 2][...],
                    probes[h * NPART // 2 : (h + 1) * NPART // 2, :WIDTH],
                    (((1,), (1,)), ((), ())),
                    preferred_element_type=f32,
                )
            )
            if b < GRID - 1:
                first, end = h * HALF // 2, (h + 1) * HALF // 2
                shift_block(b - 1, tab_ref, base, shifted[(b + 1) % 2], first, end)
        cross = jnp.concatenate(cross, axis=1)
        best = jnp.full((8, NPART), EXCLUDED, f32)
        for gx in range(GRID):
            at = (b * GRID + gx) * PAD
            score = (cross[gx * PAD : (gx + 1) * PAD] - half_energy) * SCALE
            score = jnp.where(keep, score, EXCLUDED)
            expo_ref[at : at + PAD, :] = score
            best = jnp.maximum(best, jnp.max(score.reshape(PAD // 8, 8, NPART), axis=0))
        peak = jnp.max(best, axis=0, keepdims=True)
        mass = jnp.zeros((8, NPART), f32)
        for gx in range(GRID):
            at = (b * GRID + gx) * PAD
            e = jnp.where(keep, jnp.exp(expo_ref[at : at + PAD, :] - peak), 0.0)
            expo_ref[at : at + PAD, :] = e
            mass = mass + jnp.sum(e.reshape(PAD // 8, 8, NPART), axis=0)
        stat_ref[b : b + 1, :] = peak
        stat_ref[8 + b : 9 + b, :] = jnp.sum(mass, axis=0, keepdims=True)
    peaks = [stat_ref[b : b + 1, :] for b in range(GRID)]
    peak = functools.reduce(jnp.maximum, peaks)
    stat_ref[5:6, :] = peak
    stat_ref[6:7, :] = sum(
        stat_ref[8 + b : 9 + b, :] * jnp.exp(peaks[b] - peak) for b in range(GRID)
    )


def estep(pieces, refs, table):
    return pl.pallas_call(
        estep_kernel,
        in_specs=[VMEM] * (PIECES + 5),
        out_specs=[VMEM] * 3,
        out_shape=[
            jax.ShapeDtypeStruct((NPART, WIDTH + LANES), bf16),
            jax.ShapeDtypeStruct((SHIFTS * PAD, NPART), f32),
            jax.ShapeDtypeStruct((16, NPART), f32),
        ],
        scratch_shapes=[
            pltpu.VMEM((PAD, WIDTH), f32),
            pltpu.VMEM((PAD, LANES), f32),
            pltpu.VMEM((BLOCK, WIDTH), bf16),
            pltpu.VMEM((BLOCK, WIDTH), bf16),
        ],
        compiler_params=pltpu.CompilerParams(vmem_limit_bytes=30 << 20),
        cost_estimate=pl.CostEstimate(
            flops=2 * SHIFTS * PAD * NPART * WIDTH,
            bytes_accessed=24 << 20,
            transcendentals=SHIFTS * PAD * NPART,
        ),
    )(*pieces, *refs, table)


STRIP = 256


def mstep_kernel(stat_ref, all_ref, p_ref, expo_ref, tab_ref, out_ref, post, sums):
    count = all_ref.shape[0]
    peak = all_ref[0, 0:1, :]
    for d in range(1, count):
        peak = jnp.maximum(peak, all_ref[d, 0:1, :])
    mass = jnp.zeros((1, NPART), f32)
    for d in range(count):
        mass = mass + all_ref[d, 1:2, :] * jnp.exp(all_ref[d, 0:1, :] - peak)
    inverse = 1.0 / mass
    for b in range(GRID):
        rows = slice(b * BLOCK, (b + 1) * BLOCK)
        factor = jnp.exp(stat_ref[b : b + 1, :] - peak) * inverse
        post[rows, :] = (expo_ref[rows, :] * factor).astype(bf16)
    turn = 0
    for strip in range(HALF // STRIP):
        re_cols = slice(strip * STRIP, (strip + 1) * STRIP)
        im_cols = slice(HALF + strip * STRIP, HALF + (strip + 1) * STRIP)
        for b in range(GRID):
            rows = slice(b * BLOCK, (b + 1) * BLOCK)
            k = turn % 2
            turn += 1
            sums[k, :, :STRIP] = jnp.dot(
                post[rows, :], p_ref[:, re_cols], preferred_element_type=f32
            )
            sums[k, :, STRIP:] = jnp.dot(
                post[rows, :], p_ref[:, im_cols], preferred_element_type=f32
            )
            for t in range(STRIP // LANES):
                at = strip * STRIP + t * LANES
                lanes = slice(at, at + LANES)
                res = slice(t * LANES, (t + 1) * LANES)
                ims = slice(STRIP + t * LANES, STRIP + (t + 1) * LANES)
                re = sums[k, 2 * PAD : 3 * PAD, res]
                im = sums[k, 2 * PAD : 3 * PAD, ims]
                for gx in (1, 2):
                    c = tab_ref[2 * gx - 2 : 2 * gx - 1, lanes]
                    s = tab_ref[2 * gx - 1 : 2 * gx, lanes]
                    hi = slice((2 + gx) * PAD, (3 + gx) * PAD)
                    lo = slice((2 - gx) * PAD, (3 - gx) * PAD)
                    pr, pi = sums[k, hi, res], sums[k, hi, ims]
                    mr, mi = sums[k, lo, res], sums[k, lo, ims]
                    re = re + c * (pr + mr) + s * (pi - mi)
                    im = im + c * (pi + mi) - s * (pr - mr)
                if b != 2:
                    cy, sy = y_shift(tab_ref, b - 2, lanes)
                    re, im = re * cy + im * sy, im * cy - re * sy
                g, chunk = at // CHUNK, slice(at % CHUNK, at % CHUNK + LANES)
                if b == 0:
                    out_ref[g, :, chunk] = re
                    out_ref[g + 4, :, chunk] = im
                else:
                    out_ref[g, :, chunk] += re
                    out_ref[g + 4, :, chunk] += im


def mstep(stat, stats, probes, expo, table):
    return pl.pallas_call(
        mstep_kernel,
        in_specs=[VMEM] * 5,
        out_specs=VMEM,
        out_shape=jax.ShapeDtypeStruct((GROUP, PAD, CHUNK), f32),
        scratch_shapes=[
            pltpu.VMEM((SHIFTS * PAD, NPART), bf16),
            pltpu.VMEM((2, BLOCK, 2 * STRIP), f32),
        ],
        compiler_params=pltpu.CompilerParams(vmem_limit_bytes=20 << 20),
        cost_estimate=pl.CostEstimate(
            flops=2 * SHIFTS * PAD * NPART * WIDTH, bytes_accessed=9 << 20, transcendentals=0
        ),
    )(stat, stats, probes, expo, table)


def along_z(x, far):
    return lax.ppermute(x, "z", [(i, (i + far) % GROUP) for i in range(GROUP)])


def to_other_core(x):
    return lax.ppermute(x, "co", [(0, 1), (1, 0)])


def per_device(images, offsets, class_lists, noise_weight, references):
    own, half, table = prep(images, offsets.T, class_lists.T, noise_weight)

    part = split_refs(references)
    part = lax.all_to_all(part, "z", 0, 0).reshape(CHUNK, LANES)
    part, table = lax.optimization_barrier((part, table))
    part = jnp.concatenate([part, lax.ppermute(part, "xh", [(0, 1), (1, 0)])])
    refs = [part]
    for far in (1, 2, 3):
        refs.append(lax.ppermute(part, "y", [(i, (i + far) % 4) for i in range(4)]))

    up, down = [half], [half]
    for _ in range(3):
        up.append(along_z(up[-1], 1))
        down.append(along_z(down[-1], -1))
    cut = PARTS // 4
    mine = up[1:] + down[1:] + [along_z(up[-1][:cut], 1), along_z(down[-1][cut:], -1)]
    mine[6], mine[7], *refs = lax.optimization_barrier((mine[6], mine[7], *refs))
    pieces = [own] + mine + [to_other_core(x) for x in mine]

    probes, expo, stat = estep(pieces, refs, table)
    stats = lax.all_to_all(
        jnp.broadcast_to(stat[5:7], (32, 2, NPART)), ("z", "xl", "co"), 0, 0
    )
    sums = mstep(stat, stats, probes, expo, table)

    sums = jnp.sum(lax.all_to_all(sums, ("y", "xh"), 0, 0), axis=0)
    sums = jnp.pad(sums.T, ((0, 0), (0, LANES - PAD))).reshape(GROUP, 48, LANES)
    sums = lax.all_to_all(sums, "z", 0, 0)[:, :, :ROWS]
    return jnp.transpose(sums, (1, 0, 2)).reshape(48, GROUP * ROWS)


def solution(mesh):
    fine = Mesh(mesh.devices.reshape(4, 2, 8, 2, 2), AXES)
    dom, cls = ("y", "xh", "z"), ("xl", "co")
    in_specs = (P(dom, None), P(dom, None), P(dom, None), P(), P(cls, None, dom))
    return jax.shard_map(
        per_device, mesh=fine, in_specs=in_specs, out_specs=P(dom, cls), check_vma=False
    )
```
